32 devices in a mesh: seq: 16 (over z, x, core), mp: 2 (over y).
Axes of the slice: x: 2, y: 2, z: 4, core: 2. Of those that a mesh axis runs over, the one named last changes fastest.
Arguments:
- tokens: bfloat16 [1, 4096, 1024], P(None, 'seq'), may hold values from -6 to 6
- prompt_embed: bfloat16 [1, 128, 4096], replicated, may hold values from -6 to 6
- out_grad: bfloat16 [1, 4096, 1024], P(None, 'seq'), may hold values from -6 to 6
- norm_self: float32 [1024], replicated, may hold values from 0.25 to 1.75
- w_query: bfloat16 [1024, 1024], P(None, 'mp'), may hold values from -0.1875 to 0.1875
- w_key: bfloat16 [1024, 1024], P(None, 'mp'), may hold values from -0.1875 to 0.1875
- w_value: bfloat16 [1024, 1024], P(None, 'mp'), may hold values from -0.1875 to 0.1875
- w_out: bfloat16 [1024, 1024], P('mp'), may hold values from -0.75 to 0.75
- norm_cross: float32 [1024], replicated, may hold values from 0.25 to 1.75
- c_query: bfloat16 [1024, 1024], P(None, 'mp'), may hold values from -0.1875 to 0.1875
- c_key: bfloat16 [4096, 1024], P(None, 'mp'), may hold values from -0.09375 to 0.09375
- c_value: bfloat16 [4096, 1024], P(None, 'mp'), may hold values from -0.09375 to 0.09375
- c_out: bfloat16 [1024, 1024], P('mp'), may hold values from -0.375 to 0.375
- norm_feed: float32 [1024], replicated, may hold values from 0.25 to 1.75
- w_up: bfloat16 [1024, 4096], P(None, 'mp'), may hold values from -0.1875 to 0.1875
- b_up: float32 [4096], P('mp'), may hold values from -3 to 3
- w_down: bfloat16 [4096, 1024], P('mp'), may hold values from -0.09375 to 0.09375
- b_down: float32 [1024], replicated, may hold values from -3 to 3
- timesteps: int32 [1], replicated, may hold values from 0 to 999
- crop_feats: bfloat16 [1, 256, 256, 256], P(None, 'seq', 'mp'), may hold values from -15 to 15
- crop_grad_in: bfloat16 [1, 256, 256, 256], P(None, 'seq', 'mp'), may hold values from -15 to 15
- crop_gain_one: float32 [256], P('mp'), may hold values from 0.25 to 1.75
- crop_conv_one: bfloat16 [3, 3, 256, 256], P(None, None, None, 'mp'), may hold values from -0.125 to 0.125
- crop_time: bfloat16 [1024, 256], P(None, 'mp'), may hold values from -0.1875 to 0.1875
- crop_gain_two: float32 [256], P('mp'), may hold values from 0.25 to 1.75
- crop_conv_two: bfloat16 [3, 3, 256, 256], P(None, None, 'mp'), may hold values from -0.25 to 0.25
- mid_feats: bfloat16 [1, 128, 256, 128], P(None, 'seq', 'mp'), may hold values from -15 to 15
- mid_grad_in: bfloat16 [1, 128, 256, 128], P(None, 'seq', 'mp'), may hold values from -15 to 15
- mid_gain_one: float32 [256], P('mp'), may hold values from 0.25 to 1.75
- mid_conv_one: bfloat16 [3, 3, 256, 256], P(None, None, None, 'mp'), may hold values from -0.125 to 0.125
- mid_time: bfloat16 [1024, 256], P(None, 'mp'), may hold values from -0.1875 to 0.1875
- mid_gain_two: float32 [256], P('mp'), may hold values from 0.25 to 1.75
- mid_conv_two: bfloat16 [3, 3, 256, 256], P(None, None, 'mp'), may hold values from -0.25 to 0.25
Outputs:
- output: bfloat16 [1, 4096, 1024], P(None, 'seq')
- grad_tokens: float32 [1, 4096, 1024], P(None, 'seq')
- grad_norm_self: float32 [1024], replicated
- grad_query: float32 [1024, 1024], P(None, 'mp')
- grad_key: float32 [1024, 1024], P(None, 'mp')
- grad_value: float32 [1024, 1024], P(None, 'mp')
- grad_out: float32 [1024, 1024], P('mp')
- grad_norm_cross: float32 [1024], replicated
- grad_cquery: float32 [1024, 1024], P(None, 'mp')
- grad_ckey: float32 [4096, 1024], P(None, 'mp')
- grad_cvalue: float32 [4096, 1024], P(None, 'mp')
- grad_cout: float32 [1024, 1024], P('mp')
- grad_norm_feed: float32 [1024], replicated
- grad_up: float32 [1024, 4096], P(None, 'mp')
- grad_up_bias: float32 [4096], P('mp')
- grad_down: float32 [4096, 1024], P('mp')
- grad_down_bias: float32 [1024], replicated
- crop_out: bfloat16 [1, 256, 256, 256], P(None, 'seq', 'mp')
- grad_crop: float32 [1, 256, 256, 256], P(None, 'seq', 'mp')
- grad_crop_gain_one: float32 [256], P('mp')
- grad_crop_conv_one: float32 [3, 3, 256, 256], P(None, None, None, 'mp')
- grad_crop_time: float32 [1024, 256], P(None, 'mp')
- grad_crop_gain_two: float32 [256], P('mp')
- grad_crop_conv_two: float32 [3, 3, 256, 256], P(None, None, 'mp')
- mid_out: bfloat16 [1, 128, 256, 128], P(None, 'seq', 'mp')
- grad_mid: float32 [1, 128, 256, 128], P(None, 'seq', 'mp')
- grad_mid_gain_one: float32 [256], P('mp')
- grad_mid_conv_one: float32 [3, 3, 256, 256], P(None, None, None, 'mp')
- grad_mid_time: float32 [1024, 256], P(None, 'mp')
- grad_mid_gain_two: float32 [256], P('mp')
- grad_mid_conv_two: float32 [3, 3, 256, 256], P(None, None, 'mp')
The draws below stay inside these ranges and needn't reach their ends.
All inputs are finite; a program needn't handle non-finite values.
Results may differ from the reference program's by a relative error of at most 0.025.
Values may be sent and summed in bfloat16 or wider, within the bound.
A program may use at most 320 MiB of HBM per device.

```python
import math
import jax
import jax.numpy as jnp
from jax import lax

D = 1024
HEADS = 16
FF = 4096
TD = 4096
CH = 256
GROUPS = 32
TEMB = 1024
TT = 128
GRID = 64
CROP = 256
MID = 128
IMGS = 1


def ramp_field(key, side, low_end, shift):
    noise_key, offset_key = jax.random.split(key)
    noise = jnp.clip(jax.random.normal(noise_key, (IMGS, side, CH, side), jnp.float32), -4.0, 4.0)
    offset = jax.random.uniform(offset_key, (IMGS, 1, CH, 1), jnp.float32, -shift, shift)
    ramp = low_end + (3.0 - low_end) * jnp.arange(side, dtype=jnp.float32)[None, :, None, None] / (side - 1)
    return (ramp * (noise + offset)).astype(jnp.bfloat16)


def draw_crop_feats(key, part):
    key = jax.random.fold_in(key, 3)
    return ramp_field(key, CROP, 1.0, 1.0)


def draw_crop_grad_in(key, part):
    key = jax.random.fold_in(key, 5)
    return ramp_field(key, CROP, 1.0, 1.0)


def draw_mid_feats(key, part):
    key = jax.random.fold_in(key, 7)
    return ramp_field(key, MID, 1.0, 1.0)


def draw_mid_grad_in(key, part):
    key = jax.random.fold_in(key, 11)
    return ramp_field(key, MID, 1.0, 1.0)


def block_levels(key, dims, shards, smallest, high):
    def one(axis_at, parts):
        steps = jax.random.uniform(jax.random.fold_in(jax.random.fold_in(key, 6), axis_at), (parts,), jnp.float32, smallest / len(shards), high / len(shards))
        return jnp.repeat(jnp.exp(steps), dims[axis_at] // parts).reshape((-1,) + (1,) * (len(dims) - axis_at - 1))

    level = one(*shards[0])
    for cut in shards[1:]:
        level = level * one(*cut)
    return level


def gaussian(stream_key, extent, scale, reach, cuts=(), kind=jnp.bfloat16):
    array = scale * jax.random.normal(stream_key, extent, jnp.float32)
    if cuts:
        array = array * block_levels(stream_key, extent, cuts, -0.22, 0.18)
    return jnp.clip(array, -reach, reach).astype(kind)


def setup_inputs(seed: int = 0) -> dict:
    seeds = jax.random.split(jax.random.key(seed), 34)
    return {
        "tokens": gaussian(seeds[0], (IMGS, GRID * GRID, D), 1.0, 6.0, ((1, 16),)),
        "prompt_embed": gaussian(seeds[1], (IMGS, TT, TD), 1.0, 6.0),
        "out_grad": gaussian(seeds[2], (IMGS, GRID * GRID, D), 1.0, 6.0, ((1, 16),)),
        "norm_self": jnp.clip(1.0 + 0.15 * jax.random.normal(seeds[3], (D,), jnp.float32), 0.25, 1.75),
        "w_query": gaussian(seeds[4], (D, D), D ** -0.5, 0.1875, ((1, 2),)),
        "w_key": gaussian(seeds[5], (D, D), D ** -0.5, 0.1875, ((1, 2),)),
        "w_value": gaussian(seeds[6], (D, D), D ** -0.5, 0.1875, ((1, 2),)),
        "w_out": gaussian(seeds[7], (D, D), (D // 16) ** -0.5, 0.75, ((0, 2),)),
        "norm_cross": jnp.clip(1.0 + 0.15 * jax.random.normal(seeds[8], (D,), jnp.float32), 0.25, 1.75),
        "c_query": gaussian(seeds[9], (D, D), D ** -0.5, 0.1875, ((1, 2),)),
        "c_key": gaussian(seeds[10], (TD, D), TD ** -0.5, 0.09375, ((1, 2),)),
        "c_value": gaussian(seeds[11], (TD, D), TD ** -0.5, 0.09375, ((1, 2),)),
        "c_out": gaussian(seeds[12], (D, D), (D // 4) ** -0.5, 0.375, ((0, 2),)),
        "norm_feed": jnp.clip(1.0 + 0.15 * jax.random.normal(seeds[13], (D,), jnp.float32), 0.25, 1.75),
        "w_up": gaussian(seeds[14], (D, FF), D ** -0.5, 0.1875, ((1, 2),)),
        "b_up": gaussian(seeds[15], (FF,), 0.5, 3.0, ((0, 2),), jnp.float32),
        "w_down": gaussian(seeds[16], (FF, D), FF ** -0.5, 0.09375, ((0, 2),)),
        "b_down": gaussian(seeds[17], (D,), 0.5, 3.0, (), jnp.float32),
        "timesteps": jax.random.randint(seeds[18], (IMGS,), 0, 1000).astype(jnp.int32),
        "crop_feats": draw_crop_feats(jax.random.fold_in(seeds[33], 71), 0),
        "crop_grad_in": draw_crop_grad_in(jax.random.fold_in(seeds[33], 71), 0),
        "crop_gain_one": jnp.clip(1.0 + 0.15 * jax.random.normal(seeds[21], (CH,), jnp.float32), 0.25, 1.75),
        "crop_conv_one": gaussian(seeds[22], (3, 3, CH, CH), (9 * CH) ** -0.5, 0.125, ((3, 2),)),
        "crop_time": gaussian(seeds[23], (TEMB, CH), TEMB ** -0.5, 0.1875, ((1, 2),)),
        "crop_gain_two": jnp.clip(1.0 + 0.15 * jax.random.normal(seeds[24], (CH,), jnp.float32), 0.25, 1.75),
        "crop_conv_two": gaussian(seeds[25], (3, 3, CH, CH), (9 * CH // 4) ** -0.5, 0.25, ((2, 2),)),
        "mid_feats": draw_mid_feats(jax.random.fold_in(seeds[33], 71), 0),
        "mid_grad_in": draw_mid_grad_in(jax.random.fold_in(seeds[33], 71), 0),
        "mid_gain_one": jnp.clip(1.0 + 0.15 * jax.random.normal(seeds[28], (CH,), jnp.float32), 0.25, 1.75),
        "mid_conv_one": gaussian(seeds[29], (3, 3, CH, CH), (9 * CH) ** -0.5, 0.125, ((3, 2),)),
        "mid_time": gaussian(seeds[30], (TEMB, CH), TEMB ** -0.5, 0.1875, ((1, 2),)),
        "mid_gain_two": jnp.clip(1.0 + 0.15 * jax.random.normal(seeds[31], (CH,), jnp.float32), 0.25, 1.75),
        "mid_conv_two": gaussian(seeds[32], (3, 3, CH, CH), (9 * CH // 4) ** -0.5, 0.25, ((2, 2),)),
    }


@jax.custom_vjp
def low(v):
    return lax.optimization_barrier(v.astype(jnp.bfloat16)).astype(jnp.float32)

@jax.custom_vjp
def low_back(v):
    return v

def low_keep(v):
    return (low(v), None)

def low_pass(kept, grad):
    return (grad,)

def back_keep(v):
    return (v, None)

def back_low(kept, grad):
    return (low(grad),)
low.defvjp(low_keep, low_pass)
low_back.defvjp(back_keep, back_low)
HIGHEST = lax.Precision.HIGHEST

def layer_norm(values):
    center = values - lax.optimization_barrier(jnp.mean(values, axis=-1, keepdims=True))
    spread = lax.optimization_barrier(jnp.mean(center * center, axis=-1, keepdims=True))
    return center * lax.rsqrt(spread + 1e-05)

def matmul(left, right):
    return jnp.einsum('...k,kn->...n', left, right, precision=HIGHEST)

def attend_block(query, keys, values, scale):
    scores = low_back(jnp.einsum('iqhe,ikhe->ihqk', query, keys, precision=HIGHEST) * scale)
    probs = low(jax.nn.softmax(scores, axis=-1))
    return jnp.einsum('ihqk,ikhe->iqhe', probs, values, precision=HIGHEST)

def time_features(steps, width):
    half = width // 2
    freqs = jnp.exp(-math.log(10000.0) * jnp.arange(half, dtype=jnp.float32) / half)
    angles = steps.astype(jnp.float32)[:, None] * freqs[None, :]
    return jax.nn.silu(jnp.concatenate([jnp.cos(angles), jnp.sin(angles)], axis=1))

def group_norm(values, gain):
    height, chans, width = values.shape
    grouped = values.reshape(height, GROUPS, chans // GROUPS, width)
    center = grouped - lax.optimization_barrier(jnp.mean(grouped, axis=(0, 2, 3), keepdims=True))
    spread = lax.optimization_barrier(jnp.mean(center * center, axis=(0, 2, 3), keepdims=True))
    return (center * lax.rsqrt(spread + 1e-05)).reshape(values.shape) * gain[None, :, None]

def conv_same(values, weight):
    result = lax.conv_general_dilated(values[None], weight, (1, 1), ((1, 1), (1, 1)), dimension_numbers=('NHCW', 'HWIO', 'NHCW'), precision=HIGHEST)
    return result[0]

def res_block(image, feature, gain_one, conv_one, time_weight, gain_two, conv_two):
    first = low(jax.nn.silu(group_norm(image, gain_one)))
    shift = jnp.dot(feature, time_weight, precision=HIGHEST)
    hidden = low_back(conv_same(first, conv_one)) + shift[None, :, None]
    second = low(jax.nn.silu(group_norm(hidden, gain_two)))
    return image + low_back(conv_same(second, conv_two))

def block_grads(feats, cotangent, features, params):

    def one(carry, item):
        image, grad_image, feature = item

        def run(values, *weights):
            return res_block(values, feature, *weights)
        result, back = jax.vjp(run, image.astype(jnp.float32), *params)
        grads = back(grad_image.astype(jnp.float32))
        summed = tuple((total + part for total, part in zip(carry, grads[1:])))
        return (summed, (result.astype(jnp.bfloat16), grads[0]))
    start = tuple((jnp.zeros_like(weight) for weight in params))
    totals, (results, input_grads) = lax.scan(one, start, (feats, cotangent, features))
    return (results, input_grads, totals)

def reference(tokens, prompt_embed, out_grad, norm_self, w_query, w_key, w_value, w_out, norm_cross, c_query, c_key, c_value, c_out, norm_feed, w_up, b_up, w_down, b_down, timesteps, crop_feats, crop_grad_in, crop_gain_one, crop_conv_one, crop_time, crop_gain_two, crop_conv_two, mid_feats, mid_grad_in, mid_gain_one, mid_conv_one, mid_time, mid_gain_two, mid_conv_two):
    head_dim = D // HEADS
    scale = head_dim ** (-0.5)
    length = GRID * GRID
    block = min(512, length)
    prompt = prompt_embed.astype(jnp.float32)

    def to_heads(values):
        return values.reshape(values.shape[0], values.shape[1], HEADS, head_dim)

    def self_attention(query, keys, values):
        images = query.shape[0]
        blocks = query.reshape(images, length // block, block, HEADS, head_dim).transpose(1, 0, 2, 3, 4)
        outs = lax.map(jax.checkpoint(lambda piece: attend_block(piece, keys, values, scale)), blocks)
        return outs.transpose(1, 0, 2, 3, 4).reshape(images, length, D)

    def forward(inputs, g_one, wq, wk, wv, wo, g_two, cq, ck, cv, co, g_three, wu, bu, wd, bd):
        first = low(layer_norm(inputs) * g_one)
        query = low_back(low(matmul(first, wq)))
        keys = low_back(low(matmul(first, wk)))
        values = low_back(low(matmul(first, wv)))
        mixed = low_back(low(self_attention(to_heads(query), to_heads(keys), to_heads(values))))
        after_one = inputs + low_back(matmul(mixed, wo))
        second = low(layer_norm(after_one) * g_two)
        query_two = low_back(low(matmul(second, cq)))
        keys_two = low(matmul(prompt, ck))
        values_two = low(matmul(prompt, cv))
        mixed_two = attend_block(to_heads(query_two), to_heads(keys_two), to_heads(values_two), scale)
        mixed_two = low_back(low(mixed_two.reshape(mixed_two.shape[0], length, D)))
        after_two = after_one + low_back(matmul(mixed_two, co))
        third = low(layer_norm(after_two) * g_three)
        hidden = low_back(matmul(third, wu) + bu)
        units = low(jax.nn.gelu(hidden, approximate=False))
        return after_two + low_back(matmul(units, wd)) + bd
    params = (tokens.astype(jnp.float32), norm_self, w_query.astype(jnp.float32), w_key.astype(jnp.float32), w_value.astype(jnp.float32), w_out.astype(jnp.float32), norm_cross, c_query.astype(jnp.float32), c_key.astype(jnp.float32), c_value.astype(jnp.float32), c_out.astype(jnp.float32), norm_feed, w_up.astype(jnp.float32), b_up, w_down.astype(jnp.float32), b_down)
    output, back = jax.vjp(forward, *params)
    grads = back(out_grad.astype(jnp.float32))
    features = time_features(timesteps, TEMB)
    crop_params = (crop_gain_one, crop_conv_one.astype(jnp.float32), crop_time.astype(jnp.float32), crop_gain_two, crop_conv_two.astype(jnp.float32))
    crop_out, grad_crop, crop_set = block_grads(crop_feats, crop_grad_in, features, crop_params)
    mid_params = (mid_gain_one, mid_conv_one.astype(jnp.float32), mid_time.astype(jnp.float32), mid_gain_two, mid_conv_two.astype(jnp.float32))
    mid_out, grad_mid, mid_set = block_grads(mid_feats, mid_grad_in, features, mid_params)
    return (output.astype(jnp.bfloat16), grads[0], grads[1], grads[2], grads[3], grads[4], grads[5], grads[6], grads[7], grads[8], grads[9], grads[10], grads[11], grads[12], grads[13], grads[14], grads[15], crop_out, grad_crop, crop_set[0], crop_set[1], crop_set[2], crop_set[3], crop_set[4], mid_out, grad_mid, mid_set[0], mid_set[1], mid_set[2], mid_set[3], mid_set[4])
```

```python
from functools import partial
import math

import jax
import jax.numpy as jnp
from jax import lax
from jax.experimental import pallas as pl
from jax.experimental.pallas import tpu as pltpu
from jax.sharding import PartitionSpec as P

D = 1024
HEADS = 16
GROUPS = 32
E = D // HEADS
SCALE = E ** (-0.5)
COEF = SCALE * math.log2(math.e)
KEY_CHUNK = 512
VMEM_LIMIT = 60 * 1024 * 1024
RINGS = 4

HIGHEST = lax.Precision.HIGHEST
MESH = pl.DeviceIdType.MESH
F32 = jnp.float32
BF16 = jnp.bfloat16


def dot(left, right):
    return jnp.dot(left, right, preferred_element_type=F32)


def dot_nt(left, right):
    return lax.dot_general(left, right, (((1,), (1,)), ((), ())), preferred_element_type=F32)


def dot_tn(left, right):
    return lax.dot_general(left, right, (((0,), (0,)), ((), ())), preferred_element_type=F32)


def wrap(value, size):
    value = jnp.where(value < 0, value + size, value)
    return jnp.where(value >= size, value - size, value)


def turn(block):
    return block.astype(F32).T.astype(BF16)


def greet(peers):
    barrier = pltpu.get_barrier_semaphore()
    for peer in peers:
        pl.semaphore_signal(barrier, inc=1, device_id=peer, device_id_type=MESH)
    pl.semaphore_wait(barrier, len(peers))


def remote(src, dst, send_sem, recv_sem, peer):
    return pltpu.make_async_remote_copy(
        src_ref=src,
        dst_ref=dst,
        send_sem=send_sem,
        recv_sem=recv_sem,
        device_id=peer,
        device_id_type=MESH,
    )


def vmem_call(kernel, outs, scratch, collective_id, name, in_any=(), out_any=(), aliases=None):
    def call(*args):
        return pl.pallas_call(
            kernel,
            out_shape=[jax.ShapeDtypeStruct(shape, kind) for shape, kind in outs],
            in_specs=[
                pl.BlockSpec(memory_space=pl.ANY if i in in_any else pltpu.VMEM)
                for i in range(len(args))
            ],
            out_specs=[
                pl.BlockSpec(memory_space=pl.ANY if i in out_any else pltpu.VMEM)
                for i in range(len(outs))
            ],
            scratch_shapes=scratch,
            input_output_aliases=aliases or {},
            compiler_params=pltpu.CompilerParams(
                collective_id=collective_id,
                has_side_effects=True,
                vmem_limit_bytes=VMEM_LIMIT,
            ),
            name=name,
        )(*args)

    return call


def norm_parts(values):
    center = values - jnp.mean(values, axis=-1, keepdims=True)
    inverse = lax.rsqrt(jnp.mean(center * center, axis=-1, keepdims=True) + 1e-05)
    return center * inverse, inverse


def norm_back(grad, normed, inverse, gain):
    gain_grad = jnp.sum(grad * normed, axis=0, keepdims=True)
    scaled = grad * gain
    first = jnp.mean(scaled, axis=-1, keepdims=True)
    second = jnp.mean(scaled * normed, axis=-1, keepdims=True)
    return inverse * (scaled - first - normed * second), gain_grad


class Exchange:
    def __init__(self, land, send_sem, recv_sem, m):
        self.land, self.send_sem, self.recv_sem, self.m = land, send_sem, recv_sem, m
        self.me = lax.axis_index("mp")

    def peer(self, d):
        return lax.rem(self.me + d, self.m)

    def send(self, key, rows, block):
        self.land[key, self.me, rows, :] = block.astype(BF16)
        for d in range(1, self.m):
            to = self.peer(d)
            part = self.land.at[key, self.me, rows, :]
            remote(
                part, part, self.send_sem.at[key, d], self.recv_sem.at[key, self.me], {"mp": to}
            ).start()

    def wait(self, key, rows):
        for d in range(1, self.m):
            src = self.peer(d)
            part = self.land.at[key, src, rows, :]
            copy = remote(
                part, part, self.send_sem.at[key, d], self.recv_sem.at[key, src], {"mp": src}
            )
            copy.wait_send()
            copy.wait_recv()
        total = self.land[key, 0, rows, :].astype(F32)
        for j in range(1, self.m):
            total = total + self.land[key, j, rows, :].astype(F32)
        return total


def head_peers(h, g):
    me = lax.axis_index("seq")
    slot, part = lax.div(me, g), lax.rem(me, g)
    swaps = [({"seq": lax.rem(slot + d, h) * g + part}) for d in range(1, h)]
    mates = [({"seq": slot * g + lax.rem(part + d, g)}) for d in range(1, g)]
    return slot, part, swaps, mates


def lanes(index, size):
    return pl.ds(pl.multiple_of(index * size, size), size)


class Swap:
    def __init__(self, h, g, send_sem, recv_sem):
        self.h, self.g = h, g
        self.slot, self.part, _, _ = head_peers(h, g)
        self.send_sem, self.recv_sem = send_sem, recv_sem

    def other(self, d):
        return lax.rem(self.slot + d, self.h)

    def device(self, slot):
        return {"seq": slot * self.g + self.part}


def spread_heads(swap, key, source, land, width, offset):
    for d in range(1, swap.h):
        to = swap.other(d)
        remote(
            source.at[pl.ds(pl.multiple_of(to * E, E), E), :],
            land.at[:, lanes(offset + swap.slot, width)],
            swap.send_sem.at[key, d],
            swap.recv_sem.at[key, swap.slot],
            swap.device(to),
        ).start()
    land[:, lanes(offset + swap.slot, width)] = source[
        pl.ds(pl.multiple_of(swap.slot * E, E), E), :
    ]


def spread_wait(swap, key, source, land, width, offset):
    for d in range(1, swap.h):
        src = swap.other(d)
        copy = remote(
            source.at[pl.ds(pl.multiple_of(src * E, E), E), :],
            land.at[:, lanes(offset + src, width)],
            swap.send_sem.at[key, d],
            swap.recv_sem.at[key, src],
            swap.device(src),
        )
        copy.wait_send()
        copy.wait_recv()


def return_copy(swap, key, piece, land, to):
    return remote(
        piece,
        land.at[pl.ds(pl.multiple_of(swap.slot * E, E), E), :],
        swap.send_sem.at[key, to],
        swap.recv_sem.at[key, swap.slot],
        swap.device(to),
    )


def return_wait(swap, key, pieces, land):
    for d in range(1, swap.h):
        src = swap.other(d)
        copy = remote(
            pieces.at[src],
            land.at[pl.ds(pl.multiple_of(src * E, E), E), :],
            swap.send_sem.at[key, src],
            swap.recv_sem.at[key, src],
            swap.device(src),
        )
        copy.wait_send()
        copy.wait_recv()


def mate_copy(part_to, key, d, src, dst, send_sem, recv_sem, slot, part, g):
    return remote(
        src, dst, send_sem.at[key, d], recv_sem.at[key, part], {"seq": slot * g + part_to}
    )


def attn_forward_kernel(
    h,
    g,
    x_ref,
    gain_ref,
    wq_ref,
    wk_ref,
    wv_ref,
    h1_ref,
    qh_ref,
    kv_ref,
    log_ref,
    ah_ref,
    mix_ref,
    local,
    q_land,
    kv_land,
    keys,
    mix_land,
    pieces,
    send_sem,
    recv_sem,
    mate_send,
    mate_recv,
):
    tokens = x_ref.shape[0]
    width = h * tokens
    slot, part, swaps, mates = head_peers(h, g)
    greet(swaps + mates)
    swap = Swap(h, g, send_sem, recv_sem)

    normed, _ = norm_parts(x_ref[...].astype(F32))
    first = (normed * gain_ref[...]).astype(BF16)
    h1_ref[...] = first
    for key, weight in enumerate((wk_ref, wv_ref, wq_ref)):
        local[key] = dot(first, weight[...]).T.astype(BF16)
        if key < 2:
            spread_heads(swap, key, local.at[key], kv_land.at[key], tokens, part * h)
        else:
            spread_heads(swap, key, local.at[key], q_land, tokens, 0)

    for key in range(2):
        spread_wait(swap, key, local.at[key], kv_land.at[key], tokens, part * h)
        mine = kv_land.at[key, :, lanes(part, width)]
        for d in range(1, g):
            mate_copy(
                lax.rem(part + d, g), key, d, mine, mine, mate_send, mate_recv, slot, part, g
            ).start()
    spread_wait(swap, 2, local.at[2], q_land, tokens, 0)
    for key in range(2):
        for d in range(1, g):
            src = lax.rem(part + d, g)
            theirs = kv_land.at[key, :, lanes(src, width)]
            copy = remote(
                theirs,
                theirs,
                mate_send.at[key, d],
                mate_recv.at[key, src],
                {"seq": slot * g + src},
            )
            copy.wait_send()
            copy.wait_recv()

    chunks = g * width // KEY_CHUNK

    @pl.loop(0, chunks)
    def _(c):
        keys[lanes(c, KEY_CHUNK), :] = turn(kv_land[0, :, lanes(c, KEY_CHUNK)])

    @pl.loop(0, h)
    def _(b):
        at = lax.rem(slot + 1 + b, h)
        query = q_land[:, lanes(at, tokens)]

        def step(c, carry):
            peak, total, acc = carry
            scores = dot(keys[lanes(c, KEY_CHUNK), :], query)
            higher = jnp.maximum(peak, jnp.max(scores, axis=0, keepdims=True))
            probs = jnp.exp2((scores - higher) * COEF)
            shrink = jnp.exp2((peak - higher) * COEF)
            total = total * shrink + jnp.sum(probs, axis=0, keepdims=True)
            acc = acc * shrink + dot(kv_land[1, :, lanes(c, KEY_CHUNK)], probs.astype(BF16))
            return higher, total, acc

        start = (
            jnp.full((1, tokens), -jnp.inf, F32),
            jnp.zeros((1, tokens), F32),
            jnp.zeros((E, tokens), F32),
        )
        peak, total, acc = lax.fori_loop(0, chunks, step, start)
        mixed = acc / total
        log_ref[at] = peak * COEF + jnp.log2(total)
        ah_ref[:, lanes(at, tokens)] = mixed
        pieces[at] = mixed.astype(BF16)

        @pl.when(b < h - 1)
        def _():
            return_copy(swap, 3, pieces.at[at], mix_land, at).start()

    mix_land[pl.ds(pl.multiple_of(slot * E, E), E), :] = pieces[slot]
    qh_ref[...] = q_land[...]
    kv_ref[...] = kv_land[...]
    return_wait(swap, 3, pieces, mix_land)
    mix_ref[...] = mix_land[...]


def attn_forward(tokens, gain, wq, wk, wv, n):
    rows, local = tokens.shape[0], wq.shape[1]
    h = local // E
    g = n // h
    width = h * rows
    return vmem_call(
        partial(attn_forward_kernel, h, g),
        [
            ((rows, D), BF16),
            ((E, width), BF16),
            ((2, E, g * width), BF16),
            ((h, 1, rows), F32),
            ((E, width), F32),
            ((local, rows), BF16),
        ],
        [
            pltpu.VMEM((3, local, rows), BF16),
            pltpu.VMEM((E, width), BF16),
            pltpu.VMEM((2, E, g * width), BF16),
            pltpu.VMEM((g * width, E), BF16),
            pltpu.VMEM((local, rows), BF16),
            pltpu.VMEM((h, E, rows), BF16),
            pltpu.SemaphoreType.DMA((4, h)),
            pltpu.SemaphoreType.DMA((4, h)),
            pltpu.SemaphoreType.DMA((2, g)),
            pltpu.SemaphoreType.DMA((2, g)),
        ],
        1,
        "attn_forward",
    )(tokens, gain, wq, wk, wv)


class SeqSum:
    def __init__(self, source, land, total, send_sem, recv_sem, n):
        self.source, self.land, self.total = source, land, total
        self.send_sem, self.recv_sem, self.n = send_sem, recv_sem, n
        self.rows = source.shape[0] // n
        self.fits = source.shape[0] % (8 * n) == 0
        self.me = lax.axis_index("seq")

    def block(self, at):
        return pl.ds(pl.multiple_of(at * self.rows, 8), self.rows)

    def back_copy(self, there, owner):
        part = self.total.at[self.block(owner)]
        return remote(part, part, self.send_sem.at[1], self.recv_sem.at[1], {"seq": there})

    def scatter(self):
        @pl.loop(1, self.n)
        def _(d):
            there = wrap(self.me + d, self.n)
            remote(
                self.source.at[self.block(there)],
                self.land.at[self.me],
                self.send_sem.at[0],
                self.recv_sem.at[0],
                {"seq": there},
            ).start()

        self.land[self.me] = self.source[self.block(self.me), :]

    def gather(self):
        rest = pl.ds(0, self.n - 1)
        copy = remote(
            self.land.at[rest],
            self.land.at[rest],
            self.send_sem.at[0],
            self.recv_sem.at[0],
            {"seq": self.me},
        )
        copy.wait_send()
        copy.wait_recv()
        total = self.land[0]
        for j in range(1, self.n):
            total = total + self.land[j]
        self.total[self.block(self.me), :] = total

        @pl.loop(1, self.n)
        def _(d):
            self.back_copy(wrap(self.me + d, self.n), self.me).start()

    def finish(self):
        part = self.total.at[pl.ds(0, (self.n - 1) * self.rows)]
        copy = remote(part, part, self.send_sem.at[1], self.recv_sem.at[1], {"seq": self.me})
        copy.wait_send()
        copy.wait_recv()


def attn_backward_kernel(
    h,
    g,
    m,
    units,
    ga_ref,
    qh_ref,
    kv_ref,
    log_ref,
    ah_ref,
    h1_ref,
    x_ref,
    gain_ref,
    wq_ref,
    wk_ref,
    wv_ref,
    after_ref,
    base_ref,
    partial_ref,
    text_ref,
    _,
    out_ref,
    final_ref,
    dgain_ref,
    text_out_ref,
    packed_ref,
    done_ref,
    ga_land,
    rows_kv,
    sums,
    pieces,
    halves,
    half_land,
    kv_pieces,
    land,
    cross,
    send_sem,
    recv_sem,
    mate_send,
    mate_recv,
    cross_send,
    cross_recv,
    text_land,
    text_total,
    text_send,
    text_recv,
    dqkv,
    dqkv_sem,
    *ring_scratch,
):
    tokens = x_ref.shape[0]
    width = h * tokens
    n = h * g
    local = ga_ref.shape[0]
    slot, part, swaps, mates = head_peers(h, g)
    me, here = lax.axis_index("seq"), lax.axis_index("mp")
    greet(
        [{"seq": lax.rem(me + d, n)} for d in range(1, n)]
        + [{"mp": lax.rem(here + d, m)} for d in range(1, m)]
    )
    swap = Swap(h, g, send_sem, recv_sem)
    mp_sum = Exchange(cross, cross_send, cross_recv, m)

    spread_heads(swap, 0, ga_ref, ga_land, tokens, 0)
    everything = pl.ds(0, tokens)
    mp_sum.send(1, everything, partial_ref[...])
    piece = done_ref.shape[0] // (RINGS * n)
    ring = RingSum(n, piece, True, packed_ref, done_ref, ring_scratch)
    ring.start()
    text_sum = SeqSum(text_ref, text_land, text_total, text_send, text_recv, n)
    if text_sum.fits:
        text_sum.scatter()
    chunks = g * width // KEY_CHUNK

    @pl.loop(0, chunks)
    def _(c):
        for key in range(2):
            rows_kv[key, lanes(c, KEY_CHUNK), :] = turn(kv_ref[key, :, lanes(c, KEY_CHUNK)])
            sums[key, lanes(c, KEY_CHUNK), :] = jnp.zeros((KEY_CHUNK, E), F32)

    spread_wait(swap, 0, ga_ref, ga_land, tokens, 0)
    ring.first()
    in_loop = chunks % 2 == 0 and 2 * h <= ring.ticks_all
    ring.next = 2 * h if in_loop else 0

    def one_block(b):
        at = lax.rem(slot + 1 + b, h)
        query = qh_ref[:, lanes(at, tokens)]
        grad = ga_land[:, lanes(at, tokens)]
        query_rows, grad_rows = turn(query), turn(grad)
        level = log_ref[at]
        inner = jnp.sum(grad.astype(F32) * ah_ref[:, lanes(at, tokens)], axis=0, keepdims=True)

        def step(c, acc):
            here_rows = lanes(c, KEY_CHUNK)
            scores = dot(rows_kv[0, here_rows, :], query)
            probs = jnp.exp2(scores * COEF - level)
            grad_probs = dot(rows_kv[1, here_rows, :], grad)
            grad_scores = (probs * (grad_probs - inner)).astype(BF16)
            sums[0, here_rows, :] += dot(grad_scores, query_rows)
            sums[1, here_rows, :] += dot(probs.astype(BF16), grad_rows)
            return acc + dot(kv_ref[0, :, here_rows], grad_scores)

        acc = jnp.zeros((E, tokens), F32)
        for k in range(2):
            acc = lax.fori_loop(k * chunks // 2, (k + 1) * chunks // 2, step, acc)
            if in_loop:
                ring.tick(2 * b + k)
        pieces[at] = (acc * SCALE).astype(BF16)

        @pl.when(b < h - 1)
        def _():
            return_copy(swap, 1, pieces.at[at], land.at[0], at).start()

    pl.loop(0, h)(one_block)

    for key, factor in ((0, SCALE), (1, 1.0)):
        for d in range(1, g):
            to = lax.rem(part + d, g)

            @pl.loop(0, h)
            def _(i):
                block = sums[key, lanes(to * h + i, tokens), :] * factor
                halves[key, d, :, lanes(i, tokens)] = block.T.astype(BF16)

            remote(
                halves.at[key, d],
                half_land.at[key, part],
                mate_send.at[key, d],
                mate_recv.at[key, part],
                {"seq": slot * g + to},
            ).start()
    if text_sum.fits:
        text_sum.gather()
    ring.idle(3)
    for key, factor in ((0, SCALE), (1, 1.0)):
        for d in range(1, g):
            src = lax.rem(part + d, g)
            copy = remote(
                halves.at[key, d],
                half_land.at[key, src],
                mate_send.at[key, d],
                mate_recv.at[key, src],
                {"seq": slot * g + src},
            )
            copy.wait_send()
            copy.wait_recv()

        @pl.loop(0, h)
        def _(b):
            at = lax.rem(slot + 1 + b, h)
            total = (sums[key, lanes(part * h + at, tokens), :] * factor).T
            for d in range(1, g):
                src = lax.rem(part + d, g)
                total = total + half_land[key, src, :, lanes(at, tokens)].astype(F32)
            kv_pieces[key, at] = total.astype(BF16)

            @pl.when(b < h - 1)
            def _():
                return_copy(swap, 2 + key, kv_pieces.at[key, at], land.at[1 + key], at).start()

    mine = pl.ds(pl.multiple_of(slot * E, E), E)
    land[0, mine, :] = pieces[slot]
    land[1, mine, :] = kv_pieces[0, slot]
    land[2, mine, :] = kv_pieces[1, slot]
    ring.idle(3)
    return_wait(swap, 1, pieces, land.at[0])
    return_wait(swap, 2, kv_pieces.at[0], land.at[1])
    return_wait(swap, 3, kv_pieces.at[1], land.at[2])

    grads = [turn(land[key]) for key in range(3)]
    partial_sum = dot_nt(grads[0], wq_ref[...])
    partial_sum = partial_sum + dot_nt(grads[1], wk_ref[...])
    partial_sum = partial_sum + dot_nt(grads[2], wv_ref[...])
    mp_sum.send(0, everything, partial_sum)
    first = turn(h1_ref[...])
    for key in range(3):
        product = dot(first, grads[key]).astype(BF16)
        for k in range(local // 128):
            row = (key * (local // 128) + k) * D
            dqkv[row : row + D, :] = product[:, k * 128 : (k + 1) * 128]
    start = packed_sections(local, 0)[3][0] + 2 * D // 128 * units
    store = pltpu.make_async_copy(
        dqkv, packed_ref.at[pl.ds(start, dqkv.shape[0])], dqkv_sem.at[0]
    )
    store.start()
    if text_sum.fits:
        text_sum.finish()
        text_out_ref[...] = text_total[...].astype(BF16)
    else:
        text_out_ref[...] = text_ref[...].astype(BF16)
    ring.idle(4)
    final_ref[...] = (base_ref[...] + mp_sum.wait(1, everything)).astype(BF16)
    normed, inverse = norm_parts(x_ref[...].astype(F32))
    total = mp_sum.wait(0, everything)
    into, gain_grad = norm_back(total, normed, inverse, gain_ref[...])
    out_ref[...] = after_ref[...] + into
    dgain_ref[...] = gain_grad
    store.wait()
    ring.finish()


def attn_backward(ga, qh, kv, log, ah, h1, tokens, gain, wq, wk, wv, after, base, partial_out, text, packed, units, n, m):
    rows, local = tokens.shape[0], wq.shape[1]
    h = local // E
    g = n // h
    width = h * rows
    split, total = packed_split(local, units, n)
    return vmem_call(
        partial(attn_backward_kernel, h, g, m, units),
        [
            ((rows, D), F32),
            ((rows, D), BF16),
            ((1, D), F32),
            (text.shape, BF16),
            (packed.shape, BF16),
            ((split, 128), BF16),
        ],
        [
            pltpu.VMEM((E, width), BF16),
            pltpu.VMEM((2, g * width, E), BF16),
            pltpu.VMEM((2, g * width, E), F32),
            pltpu.VMEM((h, E, rows), BF16),
            pltpu.VMEM((2, g, E, width), BF16),
            pltpu.VMEM((2, g, E, width), BF16),
            pltpu.VMEM((2, h, E, rows), BF16),
            pltpu.VMEM((3, local, rows), BF16),
            pltpu.VMEM((2, m, rows, D), BF16),
            pltpu.SemaphoreType.DMA((4, h)),
            pltpu.SemaphoreType.DMA((4, h)),
            pltpu.SemaphoreType.DMA((2, g)),
            pltpu.SemaphoreType.DMA((2, g)),
            pltpu.SemaphoreType.DMA((2, m)),
            pltpu.SemaphoreType.DMA((2, m)),
            pltpu.VMEM((n, max(text.shape[0] // n, 8), text.shape[1]), F32),
            pltpu.VMEM(text.shape, F32),
            pltpu.SemaphoreType.DMA((2,)),
            pltpu.SemaphoreType.DMA((2,)),
            pltpu.VMEM((3 * local // 128 * D, 128), BF16),
            pltpu.SemaphoreType.DMA((1,)),
        ]
        + RingSum.scratch(n, split // (RINGS * n), True),
        2,
        "attn_backward",
        in_any=(15,),
        out_any=(4, 5),
        aliases={15: 4},
    )(ga, qh, kv, log, ah, h1, tokens, gain, wq, wk, wv, after, base, partial_out, text, packed)


def middle_kernel(
    m,
    mix_ref,
    x_ref,
    og_ref,
    wo_ref,
    gain2_ref,
    cq_ref,
    k2_ref,
    v2_ref,
    co_ref,
    gain3_ref,
    wu_ref,
    bu_ref,
    wd_ref,
    bd_ref,
    base_ref,
    units_sum_ref,
    after_ref,
    ga_ref,
    text_ref,
    packed_ref,
    dgain2_ref,
    dgain3_ref,
    dup_ref,
    ddown_ref,
    h2_ref,
    gq2_ref,
    a2_ref,
    go2_ref,
    go_ref,
    h3_ref,
    gz_ref,
    u_ref,
    packed,
    packed_sem,
    back_units,
    x1,
    x2,
    q2,
    probs,
    kd,
    kdt,
    vd,
    vdt,
    land,
    send_sem,
    recv_sem,
):
    here = lax.axis_index("mp")
    greet([{"mp": lax.rem(here + d, m)} for d in range(1, m)])
    mp_sum = Exchange(land, send_sem, recv_sem, m)
    total_rows = x_ref.shape[0]
    rows = total_rows // 2
    blocks = [pl.ds(b * rows, rows) for b in range(2)]
    full = pl.ds(0, rows)
    text, local = k2_ref.shape
    units = wu_ref.shape[1]
    pairs = local // 128
    chunk = min(512, units)

    mixed = turn(mix_ref[...])
    for b in range(2):
        mp_sum.send(b, full, dot(mixed[b * rows : (b + 1) * rows], wo_ref[...]))

    low_lane = lax.broadcasted_iota(jnp.int32, (text, 128), 1) < E
    for p in range(pairs):
        cols = slice(p * 128, (p + 1) * 128)
        for source, plain, turned in ((k2_ref, kd, kdt), (v2_ref, vd, vdt)):
            both = source[:, cols].astype(F32)
            stacked = jnp.concatenate(
                [jnp.where(low_lane, both, 0.0), jnp.where(low_lane, 0.0, both)], axis=0
            )
            plain[p] = stacked.astype(BF16)
            turned[p] = stacked.T.astype(BF16)

    ddown_ref[...] = jnp.sum(og_ref[...].astype(F32), axis=0, keepdims=True)
    for b in range(2):

        @pl.loop(0, units // chunk)
        def _(c):
            cols = lanes(c, chunk)
            back_units[blocks[b], cols] = dot_nt(og_ref[blocks[b], :], wd_ref[cols, :])

    for b in range(2):
        at = blocks[b]
        x1[at, :] = x_ref[at, :].astype(F32) + mp_sum.wait(b, full)
        normed, _ = norm_parts(x1[at, :])
        second = (normed * gain2_ref[...]).astype(BF16)
        h2_ref[at, :] = second
        q2[at, :] = dot(second, cq_ref[...]).astype(BF16)
        for p in range(pairs):
            cols = slice(p * 128, (p + 1) * 128)
            scores = dot(q2[at, cols], kdt[p]) * SCALE
            parts = []
            for i in range(2):
                one = scores[:, i * text : (i + 1) * text]
                expo = jnp.exp(one - jnp.max(one, axis=-1, keepdims=True))
                parts.append(expo / jnp.sum(expo, axis=-1, keepdims=True))
            prob = jnp.concatenate(parts, axis=1)
            probs[p, at, :] = prob
            a2_ref[at, cols] = dot(prob.astype(BF16), vd[p]).astype(BF16)
        mp_sum.send(2 + b, full, dot(a2_ref[at, :], co_ref[...]))

    for b in range(2):
        at = blocks[b]
        x2[at, :] = x1[at, :] + mp_sum.wait(2 + b, full)
        normed, _ = norm_parts(x2[at, :])
        h3_ref[at, :] = (normed * gain3_ref[...]).astype(BF16)

        @pl.loop(0, units // chunk)
        def _(c):
            cols = lanes(c, chunk)
            z = dot(h3_ref[at, :], wu_ref[:, cols]) + bu_ref[:, cols]
            cdf = 0.5 + 0.5 * lax.erf(z * math.sqrt(0.5))
            slope = cdf + z * (jnp.exp(z * z * -0.5) * (1.0 / math.sqrt(2.0 * math.pi)))
            u_ref[at, cols] = (z * cdf).astype(BF16)
            gz = (back_units[at, cols] * slope).astype(BF16)
            gz_ref[at, cols] = gz
            bias = jnp.sum(gz.astype(F32), axis=0, keepdims=True)
            if b == 0:
                dup_ref[:, cols] = bias
            else:
                dup_ref[:, cols] += bias

        mp_sum.send(4 + b, full, dot_nt(gz_ref[at, :], wu_ref[...]))

    for b in range(2):
        at = blocks[b]
        units_sum_ref[at, :] = dot(u_ref[at, :], wd_ref[...]).astype(BF16)
        base_ref[at, :] = x2[at, :] + bd_ref[...]

    sections = packed_sections(local, units)[:5]

    def section_copy(which):
        start, count = sections[which][0], sections[which][1] * sections[which][2]
        rows_here = pl.ds(start, count)
        return pltpu.make_async_copy(
            packed.at[rows_here], packed_ref.at[rows_here], packed_sem.at[which]
        )

    def weight_grad(which, left, right_ref):
        start, count, height = sections[which]
        step = 4 if count % 4 == 0 else 1

        @pl.loop(0, count // step)
        def _(c):
            product = dot(left, right_ref[:, lanes(c, step * 128)]).astype(BF16)
            for k in range(step):
                place = pl.multiple_of(start + (c * step + k) * height, 16)
                packed[pl.ds(place, height), :] = product[:, k * 128 : (k + 1) * 128]

        section_copy(which).start()

    weight_grad(3, turn(h3_ref[...]), gz_ref)
    weight_grad(4, turn(u_ref[...]), og_ref)

    for b in range(2):
        at = blocks[b]
        normed, inverse = norm_parts(x2[at, :])
        into, gain_grad = norm_back(mp_sum.wait(4 + b, full), normed, inverse, gain3_ref[...])
        after = og_ref[at, :].astype(F32) + into
        x2[at, :] = after
        go2 = after.astype(BF16)
        go2_ref[at, :] = go2
        ga2 = dot_nt(go2, co_ref[...]).astype(BF16)
        for p in range(pairs):
            cols = slice(p * 128, (p + 1) * 128)
            prob = probs[p, at, :]
            grad_prob = dot(ga2[:, cols], vdt[p])
            parts = []
            for i in range(2):
                half = slice(i * text, (i + 1) * text)
                one, grad_one = prob[:, half], grad_prob[:, half]
                inner = jnp.sum(one * grad_one, axis=-1, keepdims=True)
                parts.append(one * (grad_one - inner))
            grad_scores = jnp.concatenate(parts, axis=1)
            gq2_ref[at, cols] = (dot(grad_scores.astype(BF16), kd[p]) * SCALE).astype(BF16)
            both = dot(grad_scores.T.astype(BF16), q2[at, cols]) * SCALE
            key_part = jnp.where(low_lane, both[:text], both[text:])
            both = dot(prob.T.astype(BF16), ga2[:, cols])
            value_part = jnp.where(low_lane, both[:text], both[text:])
            late = slice(local + p * 128, local + (p + 1) * 128)
            if b == 0:
                text_ref[:, cols] = key_part
                text_ref[:, late] = value_part
            else:
                text_ref[:, cols] += key_part
                text_ref[:, late] += value_part
        mp_sum.send(6 + b, full, dot_nt(gq2_ref[at, :], cq_ref[...]))
        if b == 0:
            dgain3_ref[...] = gain_grad
        else:
            dgain3_ref[...] += gain_grad

    weight_grad(0, turn(h2_ref[...]), gq2_ref)
    weight_grad(1, turn(a2_ref[...]), go2_ref)
    for b in range(2):
        at = blocks[b]
        normed, inverse = norm_parts(x1[at, :])
        into, gain_grad = norm_back(mp_sum.wait(6 + b, full), normed, inverse, gain2_ref[...])
        after = x2[at, :] + into
        after_ref[at, :] = after
        go = after.astype(BF16)
        go_ref[at, :] = go
        ga_ref[:, b * rows : (b + 1) * rows] = dot_nt(go, wo_ref[...]).T.astype(BF16)
        if b == 0:
            dgain2_ref[...] = gain_grad
        else:
            dgain2_ref[...] += gain_grad
    weight_grad(2, mix_ref[...], go_ref)
    extra = slice(2 * local, 2 * local + 128)
    text_ref[:, extra] = jnp.zeros((text, 128), F32)
    row = 0
    for vector in (dgain2_ref, dgain3_ref, dup_ref, ddown_ref):
        for i in range(vector.shape[1] // 128):
            text_ref[row : row + 1, extra] = vector[:, i * 128 : (i + 1) * 128]
            row += 1
    for which in range(len(sections)):
        section_copy(which).wait()


def packed_sections(local, units):
    sections, start = [], 0
    for count, height in (
        (local // 128, D),
        (D // 128, local),
        (D // 128, local),
        (units // 128, D),
        (D // 128, units),
        (local // 128, D),
        (local // 128, D),
        (local // 128, D),
    ):
        sections.append((start, count, height))
        start += count * height
    return sections


def packed_split(local, units, n):
    start, count, height = packed_sections(local, units)[-1]
    grain = RINGS * n * 16
    total = -(-(start + count * height) // grain) * grain
    start, count, height = packed_sections(local, units)[2]
    return max((start + count * height) // grain, 1) * grain, total


def unpack(first, second, local, units):
    split = first.shape[0]
    parts = []
    for start, count, height in packed_sections(local, units):
        if start + count * height <= split:
            part = first[start : start + count * height]
        elif start >= split:
            part = second[start - split : start - split + count * height]
        else:
            part = jnp.concatenate([first[start:], second[: start - split + count * height]])
        part = part.reshape(count, height, 128)
        parts.append(part.transpose(1, 0, 2).reshape(height, count * 128).astype(F32))
    return parts


def middle(mix, tokens, og, wo, gain2, cq, k2, v2, co, gain3, wu, bu, wd, bd, n, m):
    rows, (text, local), units = tokens.shape[0], k2.shape, wu.shape[1]
    pairs = local // 128
    _, total = packed_split(local, units, n)
    mine = packed_sections(local, units)[5][0]
    return vmem_call(
        partial(middle_kernel, m),
        [
            ((rows, D), F32),
            ((rows, D), BF16),
            ((rows, D), F32),
            ((local, rows), BF16),
            ((text, 2 * local + 128), F32),
            ((total, 128), BF16),
        ],
        [
            pltpu.VMEM((1, D), F32),
            pltpu.VMEM((1, D), F32),
            pltpu.VMEM((1, units), F32),
            pltpu.VMEM((1, D), F32),
            pltpu.VMEM((rows, D), BF16),
            pltpu.VMEM((rows, local), BF16),
            pltpu.VMEM((rows, local), BF16),
            pltpu.VMEM((rows, D), BF16),
            pltpu.VMEM((rows, D), BF16),
            pltpu.VMEM((rows, D), BF16),
            pltpu.VMEM((rows, units), BF16),
            pltpu.VMEM((rows, units), BF16),
            pltpu.VMEM((mine, 128), BF16),
            pltpu.SemaphoreType.DMA((5,)),
            pltpu.VMEM((rows, units), F32),
            pltpu.VMEM((rows, D), F32),
            pltpu.VMEM((rows, D), F32),
            pltpu.VMEM((rows, local), BF16),
            pltpu.VMEM((pairs, rows, 2 * text), F32),
            pltpu.VMEM((pairs, 2 * text, 128), BF16),
            pltpu.VMEM((pairs, 128, 2 * text), BF16),
            pltpu.VMEM((pairs, 2 * text, 128), BF16),
            pltpu.VMEM((pairs, 128, 2 * text), BF16),
            pltpu.VMEM((8, m, rows // 2, D), BF16),
            pltpu.SemaphoreType.DMA((8, m)),
            pltpu.SemaphoreType.DMA((8, m)),
        ],
        3,
        "middle",
        out_any=(5,),
    )(mix, tokens, og, wo, gain2, cq, k2, v2, co, gain3, wu, bu, wd, bd)


def ring_chip(place, chips):
    if chips % 2:
        return place
    half = chips // 2
    return jnp.where(place < half, 2 * place, 2 * (chips - 1 - place) + 1)


def ring_place(chip, chips):
    if chips % 2:
        return chip
    z, x = lax.div(chip, 2), lax.rem(chip, 2)
    return jnp.where(x == 0, z, chips - 1 - z)


class RingSum:
    SCRATCH = (
        "pair",
        "land",
        "stage",
        "send_sem",
        "recv_sem",
        "pair_send",
        "pair_recv",
        "out_send",
        "out_recv",
        "stage_sem",
        "keep_sem",
    )

    @staticmethod
    def scratch(n, piece, staged):
        dma, chips = pltpu.SemaphoreType.DMA, n // 2
        return [
            pltpu.VMEM((RINGS, chips, piece, 128), BF16),
            pltpu.VMEM((RINGS, chips - 1, piece, 128), BF16),
            pltpu.VMEM((RINGS, 2, piece, 128) if staged else (1, 1, 16, 128), BF16),
            dma((RINGS, 2 * chips)),
            dma((RINGS, 2 * chips)),
            dma((RINGS, chips)),
            dma((RINGS, chips)),
            dma((RINGS, chips)),
            dma((RINGS, chips)),
            dma((RINGS, 2)),
            dma((RINGS,)),
        ]

    def __init__(self, n, piece, staged, own, done, scratch, base=0):
        self.__dict__.update(zip(self.SCRATCH, scratch))
        self.own, self.done, self.base = own, done, base
        self.piece, self.staged = piece, staged
        self.chips, self.steps = n // 2, n // 2 - 1
        me = lax.axis_index("seq")
        chip, self.core = lax.div(me, 2), lax.rem(me, 2)
        place = ring_place(chip, self.chips)
        self.mate = {"seq": 2 * chip + 1 - self.core}
        after = 2 * ring_chip(wrap(place + 1, self.chips), self.chips) + self.core
        before = 2 * ring_chip(wrap(place - 1, self.chips), self.chips) + self.core
        self.ways = [
            (place, {"seq": after}),
            (wrap(self.chips - place, self.chips), {"seq": before}),
        ]
        self.half = RINGS * self.chips * piece
        self.groups = RINGS // 2
        self.next = 0
        self.ticks_all = self.groups * (2 * self.steps - 1)

    def chunk(self, v, t):
        return wrap(v - t, self.chips)

    def rows(self, core, q, chunk, base=0):
        start = base + core * self.half + (q * self.chips + chunk) * self.piece
        return pl.ds(pl.multiple_of(start, 16), self.piece)

    def ring_copy(self, src, dst, q, t, to):
        return remote(src, dst, self.send_sem.at[q, t], self.recv_sem.at[q, t], to)

    def pair_copy(self, q, v, t):
        chunk = self.chunk(v, t)
        return remote(
            self.own.at[self.rows(1 - self.core, q, chunk, self.base)],
            self.pair.at[q, chunk],
            self.pair_send.at[q, t],
            self.pair_recv.at[q, t],
            self.mate,
        )

    def out_copy(self, src, there, q, k):
        return remote(src, there, self.out_send.at[q, k], self.out_recv.at[q, k], self.mate)

    def fetch(self, q, v, t, slot):
        return pltpu.make_async_copy(
            self.own.at[self.rows(self.core, q, self.chunk(v, t), self.base)],
            self.stage.at[q, slot],
            self.stage_sem.at[q, slot],
        )

    def keep(self, q, v):
        return pltpu.make_async_copy(
            self.land.at[q, self.steps - 1],
            self.done.at[self.rows(self.core, q, wrap(v + 1, self.chips))],
            self.keep_sem.at[q],
        )

    def mine(self, q, v, t, slot):
        chunk = self.chunk(v, t)
        if self.staged:
            self.fetch(q, v, t, slot).wait()
            part = self.stage[q, slot]
        else:
            part = self.own[self.rows(self.core, q, chunk, self.base), :]
        self.pair_copy(q, v, t).wait_recv()
        return part.astype(F32) + self.pair[q, chunk].astype(F32)

    def start(self):
        for t in range(2):
            for q in range(RINGS):
                v, _ = self.ways[q % 2]
                self.pair_copy(q, v, t).start()
                if self.staged:
                    self.fetch(q, v, t, t).start()

    def first(self):
        for q in range(RINGS):
            v, to = self.ways[q % 2]
            here = self.pair.at[q, v]
            self.pair[q, v] = self.mine(q, v, 0, 0).astype(BF16)
            self.ring_copy(here, self.land.at[q, 0], q, 0, to).start()

    def tick(self, u):
        steps = self.steps
        t = lax.div(u, self.groups) + 1
        group = lax.rem(u, self.groups)
        slot = lax.rem(t, 2)

        @pl.when(t <= steps)
        def _():
            for way in range(2):
                v, to = self.ways[way]
                q = 2 * group + way

                @pl.when(t < steps)
                def _():
                    self.pair_copy(q, v, t + 1).start()
                    if self.staged:
                        self.fetch(q, v, t + 1, 1 - slot).start()

                here = self.land.at[q, t - 1]
                mine = self.mine(q, v, t, slot)
                self.ring_copy(here, here, q, t - 1, to).wait_recv()
                self.land[q, t - 1] = (self.land[q, t - 1].astype(F32) + mine).astype(BF16)

                @pl.when(t < steps)
                def _():
                    self.ring_copy(here, self.land.at[q, t], q, t, to).start()

                @pl.when(t == steps)
                def _():
                    there = self.done.at[self.rows(self.core, q, wrap(v + 1, self.chips))]
                    self.ring_copy(here, there, q, t, to).start()
                    self.out_copy(here, there, q, 0).start()
                    self.keep(q, v).start()

        @pl.when(t > steps)
        def _():
            for way in range(2):
                v, to = self.ways[way]
                q = 2 * group + way
                k = t - steps
                part = self.done.at[self.rows(self.core, q, self.chunk(v + 1, k))]
                self.ring_copy(part, part, q, t - 1, to).wait_recv()
                self.ring_copy(part, part, q, t, to).start()
                self.out_copy(part, part, q, k).start()

    def loop(self, count, ticks, body):
        ticks = max(min(ticks, self.ticks_all - self.next, count), 0)
        if ticks == 0:
            pl.loop(0, count)(body)
            return
        first = self.next
        self.next += ticks
        every = count // ticks

        @pl.loop(0, ticks)
        def _(k):
            @pl.loop(0, every)
            def _(i):
                body(k * every + i)

            self.tick(first + k)

        if ticks * every < count:
            pl.loop(ticks * every, count)(body)

    def idle(self, count):
        count = min(count, self.ticks_all - self.next)
        first = self.next
        self.next += count
        if count:
            pl.loop(first, first + count)(self.tick)

    def finish(self):
        self.idle(self.ticks_all)
        last = 2 * self.steps
        for q in range(RINGS):
            v, to = self.ways[q % 2]
            part = self.done.at[self.rows(self.core, q, self.chunk(v + 1, self.steps))]
            self.ring_copy(part, part, q, last - 1, to).wait_recv()
            self.out_copy(part, part, q, self.steps).start()
            self.keep(q, v).wait()

        @pl.loop(0, last)
        def _(t):
            for q in range(RINGS):
                v, to = self.ways[q % 2]
                self.ring_copy(self.land.at[q, 0], self.land.at[q, 0], q, t, to).wait_send()

        @pl.loop(0, self.chips)
        def _(t):
            for q in range(RINGS):
                v, _ = self.ways[q % 2]
                self.pair_copy(q, v, t).wait_send()
                other = self.done.at[self.rows(1 - self.core, q, self.chunk(v + 1, t))]
                copy = self.out_copy(other, other, q, t)
                copy.wait_send()
                copy.wait_recv()


GROUP = 8


def fold(values):
    total = values[:, :128]
    for i in range(1, values.shape[1] // 128):
        total = total + values[:, i * 128 : (i + 1) * 128]
    return total


def wide(columns, width):
    return jnp.concatenate([columns] * (width // 128), axis=1) if width > 128 else columns


def silu_parts(scaled):
    gate = jax.nn.sigmoid(scaled)
    return scaled * gate, gate * (1.0 + scaled * (1.0 - gate))


def pack_sums(columns):
    lane = lax.broadcasted_iota(jnp.int32, (8, 128), 1)
    tile = jnp.zeros((8, 128), F32)
    for q, sums in enumerate(columns):
        groups = sums.shape[0] // GROUP
        line = jnp.sum(sums, axis=1, keepdims=True)
        for t in range(groups):
            tile = jnp.where(lane == q * groups + t, line[t * GROUP : (t + 1) * GROUP], tile)
    return tile


def unpack_sums(tile, count, channels):
    groups = channels // GROUP
    row = jnp.sum(tile, axis=0, keepdims=True)
    turned = jnp.broadcast_to(row, (128, 128)).T
    blocks = []
    for q in range(count):
        part = turned[q * groups : (q + 1) * groups]
        part = jnp.broadcast_to(part[:, None, :], (groups, GROUP, 128))
        blocks.append(part.reshape(channels, 128))
    return blocks


def put_shifted(stack, row, values):
    width = values.shape[1]
    lane = lax.broadcasted_iota(jnp.int32, values.shape, 1)
    stack[row, 0] = jnp.where(lane == 0, 0.0, pltpu.roll(values, 1, 1)).astype(BF16)
    stack[row, 1] = values.astype(BF16)
    stack[row, 2] = jnp.where(lane == width - 1, 0.0, pltpu.roll(values, width - 1, 1)).astype(BF16)


def three_rows(stack, row):
    return stack[pl.ds(row, 3)].reshape(9 * stack.shape[2], stack.shape[3])


class ConvMap:
    INPUTS = ("gain_one", "gain_two", "shift", "weight_one", "weight_two")
    OUTPUTS = ("out", "grad")
    SCRATCH = (
        "feats",
        "cot",
        "act",
        "stack_two",
        "wt1",
        "wt2",
        "wb2",
        "wb1",
        "raw",
        "hid",
        "send_both",
        "got_two",
        "got_one",
        "gains",
        "norm_one",
        "norm_two",
        "acc",
        "vec",
    )

    def __init__(self, index, n, m, sources, refs, sems):
        self.index, self.n, self.m = index, n, m
        self.sources = sources
        self.__dict__.update(refs)
        self.__dict__.update(sems)
        self.rows, self.local, self.width = self.out.shape
        self.chans = self.feats.shape[1]
        self.me, self.here = lax.axis_index("seq"), lax.axis_index("mp")
        self.high = self.rows * n
        self.count = float(self.high * self.width * GROUP)
        self.own = pl.ds(pl.multiple_of(self.here * self.local, self.local), self.local)
        self.step = max(self.rows // 4, 2)

    def ticks(self, crop, mid):
        return (crop, mid)[self.index]

    def peer(self, d):
        return lax.rem(self.here + d, self.m)

    def loads(self, which):
        full = (self.feats, self.cot)[which]
        copies = []
        for d in range(self.m):
            chans = pl.ds(pl.multiple_of(self.peer(d) * self.local, self.local), self.local)
            copies.append(
                pltpu.make_async_copy(
                    self.sources[which][d],
                    full.at[pl.ds(2, self.rows), chans, :],
                    self.load_sem.at[self.index, which, d],
                )
            )
        return copies

    def gain_copies(self):
        return [
            remote(
                self.gain_one,
                self.gains.at[self.own, :],
                self.gain_send.at[self.index, d],
                self.gain_recv.at[self.index, d],
                {"mp": self.peer(d)},
            )
            for d in range(1, self.m)
        ]

    def edges(self, which):
        full, rows = (self.feats, self.cot)[which], self.rows
        up = remote(
            full.at[pl.ds(2, 2)],
            full.at[pl.ds(rows + 2, 2)],
            self.edge_send.at[self.index, which, 0],
            self.edge_recv.at[self.index, which, 0],
            {"seq": jnp.maximum(self.me - 1, 0)},
        )
        down = remote(
            full.at[pl.ds(rows, 2)],
            full.at[pl.ds(0, 2)],
            self.edge_send.at[self.index, which, 1],
            self.edge_recv.at[self.index, which, 1],
            {"seq": jnp.minimum(self.me + 1, self.n - 1)},
        )
        return up, down

    def start_edges(self, which):
        up, down = self.edges(which)
        full, rows = (self.feats, self.cot)[which], self.rows
        blank = jnp.zeros((2,) + full.shape[1:], BF16)

        @pl.when(self.me > 0)
        def _():
            up.start()

        @pl.when(self.me == 0)
        def _():
            full[pl.ds(0, 2)] = blank

        @pl.when(self.me < self.n - 1)
        def _():
            down.start()

        @pl.when(self.me == self.n - 1)
        def _():
            full[pl.ds(rows + 2, 2)] = blank

    def wait_edges(self, which):
        up, down = self.edges(which)

        @pl.when(self.me > 0)
        def _():
            up.wait_send()
            down.wait_recv()

        @pl.when(self.me < self.n - 1)
        def _():
            down.wait_send()
            up.wait_recv()

    def stat_copy(self, key, part, there):
        return remote(
            part, part, self.stat_send.at[key], self.stat_recv.at[key], {"seq": there}
        )

    def send_stats(self, e, tile):
        key = 4 * self.index + e
        self.stat[key, self.me] = tile

        @pl.loop(1, self.n)
        def _(d):
            part = self.stat.at[key, self.me]
            self.stat_copy(key, part, wrap(self.me + d, self.n)).start()

    def sum_stats(self, e):
        key = 4 * self.index + e
        copy = self.stat_copy(key, self.stat.at[key, pl.ds(0, self.n - 1)], self.me)
        copy.wait_send()
        copy.wait_recv()
        total = self.stat[key, 0]
        for j in range(1, self.n):
            total = total + self.stat[key, j]
        return total

    def wait_stats(self, e, channels):
        return unpack_sums(self.sum_stats(e), 2, channels)

    def clear(self, count):
        for q in range(count):
            self.acc[q] = jnp.zeros(self.acc.shape[1:], F32)

    def valid(self, row):
        at = self.me * self.rows + row
        return jnp.logical_and(at >= 0, at < self.high)

    def inside(self, e):
        return jnp.logical_and(e >= 1, e <= self.rows).astype(F32)

    def wide(self, columns):
        return wide(columns, self.width)

    def lay_out_weights(self):
        chans, local = self.chans, self.local
        for i in range(3):
            for j in range(3):
                tap = 3 * i + j
                one, two = self.weight_one[i, j], self.weight_two[i, j]
                rows = slice(j * local, (j + 1) * local)
                self.wt1[rows, i * chans : (i + 1) * chans] = turn(one)
                self.wt2[:, tap * local : (tap + 1) * local] = turn(two)
                rows = slice((2 - j) * local, (3 - j) * local)
                self.wb2[rows, (2 - i) * chans : (3 - i) * chans] = two
                self.wb1[:, (8 - tap) * local : (9 - tap) * local] = one

    def row_pairs(self):
        return 256 // self.width if self.width < 256 and self.rows % 2 == 0 else 1

    def conv_all(self, weights, source, ticks, use):
        together, local, width = self.row_pairs(), self.local, self.width
        taps_in = 3 * self.chans

        def body(step):
            first = step * together
            side = [source[pl.ds(first + k, 3)].reshape(taps_in, width) for k in range(together)]
            block = jnp.concatenate(side, axis=1) if together > 1 else side[0]
            products = dot(weights[...], block)
            lane = lax.broadcasted_iota(jnp.int32, (local, width), 1)
            for k in range(together):
                cols = slice(k * width, (k + 1) * width)
                left, middle, right = [
                    products[j * local : (j + 1) * local, cols] for j in range(3)
                ]
                left = jnp.where(lane == 0, 0.0, pltpu.roll(left, 1, 1))
                right = jnp.where(lane == width - 1, 0.0, pltpu.roll(right, width - 1, 1))
                use(first + k, left + middle + right)

        self.back.loop((self.rows + 2) // together, ticks, body)

    def first_sums(self):
        self.clear(2)

        @pl.loop(0, self.rows)
        def _(y):
            values = self.feats[y + 2].astype(F32)
            self.acc[0] += fold(values)
            self.acc[1] += fold(values * values)

        self.send_stats(0, pack_sums([self.acc[0], self.acc[1]]))

    def back_two(self):
        def use(e, values):
            self.raw[e] = values

        self.conv_all(self.wb2, self.cot, self.ticks(4, 1), use)

    def norm_of(self, total, squares):
        mean = total / self.count
        return mean, lax.rsqrt(squares / self.count - mean * mean + 1e-05)

    def conv_one(self):
        mean, inverse = self.norm_of(*self.wait_stats(0, self.chans))
        self.norm_one[0], self.norm_one[1] = mean, inverse
        gains = self.gains[...]
        scale = inverse * gains
        offset = -mean * scale
        self.norm_one[2], self.norm_one[3] = scale, offset

        def activate(r):
            scaled = self.feats[r].astype(F32) * self.wide(self.norm_one[2])
            scaled = scaled + self.wide(self.norm_one[3])
            act = scaled * jax.nn.sigmoid(scaled)
            self.act[r] = jnp.where(self.valid(r - 2), act, 0.0).astype(BF16)

        self.back.loop(self.rows + 4, self.ticks(1, 1), activate)
        self.clear(2)

        def use(e, values):
            hid = values + self.wide(self.shift[...])
            self.hid[e] = hid
            mine = self.inside(e)
            self.acc[0, : self.local] += fold(hid) * mine
            self.acc[1, : self.local] += fold(hid * hid) * mine

        self.conv_all(self.wt1, self.act, self.ticks(4, 1), use)
        self.send_stats(1, pack_sums([self.acc[0, : self.local], self.acc[1, : self.local]]))

    def second_norm(self, e):
        normed = (self.hid[e] - self.wide(self.norm_two[0])) * self.wide(self.norm_two[1])
        return normed, normed * self.wide(self.gain_two[...])

    def conv_two(self):
        mean, inverse = self.norm_of(*self.wait_stats(1, self.local))
        self.norm_two[0], self.norm_two[1] = mean, inverse
        self.clear(2)

        def sweep(e):
            normed, scaled = self.second_norm(e)
            act, slope = silu_parts(scaled)
            put_shifted(self.stack_two, e, jnp.where(self.valid(e - 1), act, 0.0))
            grad = self.raw[e] * slope
            self.raw[e] = grad * self.wide(self.gain_two[...])
            mine = self.inside(e)
            self.acc[0, : self.local] += fold(grad) * mine
            self.acc[1, : self.local] += fold(grad * normed) * mine

        self.back.loop(self.rows + 2, self.ticks(2, 1), sweep)
        first, second = self.acc[0, : self.local], self.acc[1, : self.local]
        self.put_vec(1, second)
        gain = self.gain_two[...]
        self.send_stats(2, pack_sums([first * gain, second * gain]))
        for c in range(self.rows // self.step):

            self.conv_own(self.wt2, self.send_both, c * self.step, self.step)

            for copy in self.channel_copies(0, c):
                copy.start()

        self.weight_sum(self.cot, self.ticks(2, 0))
        for i in range(self.chans // 128):
            cols = slice(i * 128, (i + 1) * 128)
            self.put_taps(2 * self.index + 1, i, self.sums[:, cols].astype(BF16))

    def many_rows(self):
        return min(1024 // self.width, self.rows)

    def put_taps(self, which, block, values):
        if self.last is None:
            (self.gw1, self.gw2)[which % 2][which // 2, block] = values
        else:
            rows = values.shape[0]
            start = which * 9 * self.chans * self.local // 128 + block * rows
            self.taps[start : start + rows, :] = values

    def last_loop(self, count, ticks, body):
        if self.last is not None:
            self.last.loop(count, ticks, body)
        else:
            pl.loop(0, count)(body)

    def side_rows(self, y, together):
        side = [three_rows(self.stack_two, y + k) for k in range(together)]
        return jnp.concatenate(side, axis=1) if together > 1 else side[0]

    def conv_own(self, weights, target, start, count):
        together = self.row_pairs()

        def body(step):
            first = start + step * together
            product = dot(weights[...], self.side_rows(first, together)).astype(BF16)
            for k in range(together):
                target[first + k] = product[:, k * self.width : (k + 1) * self.width]

        self.back.loop(count // together, self.ticks(start // count % 2, start // count // 3), body)

    def put_vec(self, at, columns):
        lane = lax.broadcasted_iota(jnp.int32, (self.local, 128), 1)
        line = jnp.sum(columns, axis=1, keepdims=True)
        self.vec[...] = jnp.where(lane == at, line, self.vec[...])

    def channel_copies(self, which, c):
        out = self.send_both
        land = (self.got_two, self.got_one)[which]
        rows = pl.ds(c * self.step, self.step)
        copies = []
        for d in range(1, self.m):
            to = self.peer(d)
            chans = pl.ds(pl.multiple_of(to * self.local, self.local), self.local)
            copies.append(
                remote(
                    out.at[rows, chans, :],
                    land.at[d - 1, rows],
                    self.chan_send.at[self.index, which, d, c],
                    self.chan_recv.at[self.index, which, d, c],
                    {"mp": to},
                )
            )
        return copies

    def wait_channels(self, which):
        for c in range(self.rows // self.step):
            for copy in self.channel_copies(which, c):
                copy.wait_send()
                copy.wait_recv()

    def channel_sum(self, which, y):
        total = self.send_both[y, self.own, :].astype(F32)
        land = (self.got_two, self.got_one)[which]
        for d in range(1, self.m):
            total = total + land[d - 1, y].astype(F32)
        return total

    def back_one(self):
        first, second = self.wait_stats(2, self.local)
        self.norm_two[2], self.norm_two[3] = first / self.count, second / self.count
        self.acc[2, : self.local] = jnp.zeros((self.local, 128), F32)

        def sweep(e):
            normed, _ = self.second_norm(e)
            grad = self.raw[e] - self.wide(self.norm_two[2]) - normed * self.wide(self.norm_two[3])
            grad = jnp.where(self.valid(e - 1), grad * self.wide(self.norm_two[1]), 0.0)
            put_shifted(self.stack_two, e, grad)
            self.acc[2, : self.local] += fold(grad) * self.inside(e)

        self.back.loop(self.rows + 2, self.ticks(2, 1), sweep)
        self.put_vec(2, self.acc[2, : self.local])
        self.finish_out()
        for c in range(self.rows // self.step):

            self.conv_own(self.wb1, self.send_both, c * self.step, self.step)

            for copy in self.channel_copies(1, c):
                copy.start()

    def grad_weight_one(self):
        self.weight_sum(self.act, self.ticks(2, 0))
        for tap in range(9):
            rows = slice((8 - tap) * self.local, (9 - tap) * self.local)
            self.put_taps(2 * self.index, tap, self.sums[rows, :].T.astype(BF16))

    def weight_sum(self, source, ticks):
        together = self.many_rows()
        self.sums[...] = jnp.zeros(self.sums.shape, F32)

        def body(step):
            first = step * together
            block = jnp.concatenate([source[first + k + 2] for k in range(together)], axis=1)
            self.sums[...] += dot_nt(self.side_rows(first, together), block)

        self.back.loop(self.rows // together, ticks, body)

    def own_norm(self, y):
        mean, inverse = self.norm_one[0, self.own, :], self.norm_one[1, self.own, :]
        values = self.feats[y + 2, self.own, :].astype(F32)
        normed = (values - self.wide(mean)) * self.wide(inverse)
        return values, normed, inverse

    def last_sums(self):
        self.wait_channels(1)
        self.clear(2)

        def sweep(y):
            _, normed, _ = self.own_norm(y)
            _, slope = silu_parts(normed * self.wide(self.gain_one[...]))
            grad = self.channel_sum(1, y) * slope
            self.grad[y] = grad
            self.acc[0, : self.local] += fold(grad)
            self.acc[1, : self.local] += fold(grad * normed)

        self.last_loop(self.rows, self.ticks(5, 2), sweep)
        first, second = self.acc[0, : self.local], self.acc[1, : self.local]
        self.put_vec(0, second)
        gain = self.gain_one[...]
        self.send_stats(3, pack_sums([first * gain, second * gain]))

    def finish_out(self):
        self.wait_channels(0)

        @pl.loop(0, self.rows)
        def _(y):
            values = self.feats[y + 2, self.own, :].astype(F32)
            self.out[y] = (values + self.channel_sum(0, y)).astype(BF16)

    def finish_grad(self):
        first, second = self.wait_stats(3, self.local)
        self.norm_two[2], self.norm_two[3] = first / self.count, second / self.count

        def sweep(y):
            _, normed, inverse = self.own_norm(y)
            grad = self.grad[y] * self.wide(self.gain_one[...])
            grad = grad - self.wide(self.norm_two[2]) - normed * self.wide(self.norm_two[3])
            cot = self.cot[y + 2, self.own, :].astype(F32)
            self.grad[y] = cot + grad * self.wide(inverse)

        self.last_loop(self.rows, self.ticks(5, 2), sweep)


def conv_kernel(n, m, split, packable, *refs):
    refs = list(refs)

    def take(count):
        taken = refs[:count]
        del refs[:count]
        return taken

    own, gain_ref = take(2)
    sources, inputs = [], []
    for _ in range(2):
        sources.append((take(m), take(m)))
        inputs.append(take(len(ConvMap.INPUTS)))
    outputs = [take(len(ConvMap.OUTPUTS)) for _ in range(2)]
    vec_ref, gain_out, done = take(3)
    shared = {"last": None}
    if packable:
        last_done = take(1)[0]
    else:
        shared.update(zip(("gw1", "gw2"), take(2)))
    scratch = [take(len(ConvMap.SCRATCH)) for _ in range(2)]
    names = (
        "stat",
        "load_sem",
        "gain_send",
        "gain_recv",
        "edge_send",
        "edge_recv",
        "stat_send",
        "stat_recv",
        "chan_send",
        "chan_recv",
        "sums",
    )
    shared.update(zip(names, take(len(names))))
    piece = done.shape[0] // (RINGS * n)
    back = RingSum(n, piece, True, own, done, take(len(RingSum.SCRATCH)), split)
    shared["back"] = back
    last = None
    if packable:
        taps = take(1)[0]
        piece = taps.shape[0] // (RINGS * n)
        last = RingSum(n, piece, False, taps, last_done, take(len(RingSum.SCRATCH)))
        shared.update(taps=taps, last=last)
    maps = []
    for i in range(2):
        named = dict(zip(ConvMap.INPUTS, inputs[i]))
        named.update(zip(ConvMap.OUTPUTS, outputs[i]))
        named.update(zip(ConvMap.SCRATCH, scratch[i]))
        maps.append(ConvMap(i, n, m, sources[i], named, shared))

    for one in maps:
        for which in range(2):
            for copy in one.loads(which):
                copy.start()
    me, here = maps[0].me, maps[0].here
    greet(
        [{"seq": lax.rem(me + d, n)} for d in range(1, n)]
        + [{"mp": lax.rem(here + d, m)} for d in range(1, m)]
    )
    for one in maps:
        one.gains[one.own, :] = one.gain_one[...]
        one.vec[...] = jnp.zeros(one.vec.shape, F32)
        for copy in one.gain_copies():
            copy.start()
    for which in (1, 0):
        for one in maps:
            for copy in one.loads(which):
                copy.wait()
            one.start_edges(which)
    back.start()
    maps[1].send_stats(5, gain_ref[...])
    for one in maps:
        one.lay_out_weights()
    for one in maps:
        one.first_sums()
    back.first()
    for one in maps:
        one.wait_edges(1)
        one.back_two()
    for one in maps:
        for copy in one.gain_copies():
            copy.wait_send()
            copy.wait_recv()
        one.wait_edges(0)
        one.conv_one()
    for one in maps:
        one.conv_two()
    for one in maps:
        one.back_one()
    for one in maps:
        one.grad_weight_one()
    back.idle(back.ticks_all)
    if packable:
        rows = 4 * 9 * maps[0].chans * maps[0].local // 128
        if rows < taps.shape[0]:
            taps[rows:, :] = jnp.zeros((taps.shape[0] - rows, 128), BF16)
        last.start()
        last.first()
    for one in maps:
        one.last_sums()
    lines = [one.vec[...].T[:3] for one in maps]
    lines = jnp.concatenate(lines + [jnp.zeros((2, maps[0].local), F32)], axis=0)
    if maps[0].local < 128:
        blank = jnp.zeros((8, 128 - maps[0].local), F32)
        lines = jnp.concatenate([lines, blank], axis=1)
    maps[1].send_stats(4, lines)
    for one in maps:
        one.finish_grad()
    vec_ref[...] = maps[1].sum_stats(4)
    gain_out[...] = maps[1].sum_stats(5)
    back.finish()
    if packable:
        last.finish()


def res_blocks(maps, features, packed, vector, split, peers, n, m):
    args, in_any, outs, scratch = [packed, vector.reshape(8, 128)], [0], [], []
    for feats, cot, gain_one, conv_one, time_weight, gain_two, conv_two in maps:
        _, rows, local, width = feats.shape
        chans = conv_one.shape[2]
        for values in (feats[0], cot[0]):
            in_any += range(len(args), len(args) + m)
            args.append(values)
            args += peers.pop(0)
        shift = jnp.dot(features, time_weight.astype(F32), precision=HIGHEST)[0]
        args += [
            jnp.broadcast_to(column[:, None], (local, 128))
            for column in (gain_one, gain_two, shift)
        ]
        args += [conv_one, conv_two]
        outs += [
            ((rows, local, width), BF16),
            ((rows, local, width), F32),
        ]
        scratch += [
            pltpu.VMEM((rows + 4, chans, width), BF16),
            pltpu.VMEM((rows + 4, chans, width), BF16),
            pltpu.VMEM((rows + 4, chans, width), BF16),
            pltpu.VMEM((rows + 2, 3, local, width), BF16),
            pltpu.VMEM((3 * local, 3 * chans), BF16),
            pltpu.VMEM((chans, 9 * local), BF16),
            pltpu.VMEM((3 * local, 3 * chans), BF16),
            pltpu.VMEM((chans, 9 * local), BF16),
            pltpu.VMEM((rows + 2, local, width), F32),
            pltpu.VMEM((rows + 2, local, width), F32),
            pltpu.VMEM((rows, chans, width), BF16),
            pltpu.VMEM((m - 1, rows, local, width), BF16),
            pltpu.VMEM((m - 1, rows, local, width), BF16),
            pltpu.VMEM((chans, 128), F32),
            pltpu.VMEM((4, chans, 128), F32),
            pltpu.VMEM((4, local, 128), F32),
            pltpu.VMEM((3, chans, 128), F32),
            pltpu.VMEM((local, 128), F32),
        ]
    dma = pltpu.SemaphoreType.DMA
    rest = packed.shape[0] - split
    scratch += [
        pltpu.VMEM((10, n, 8, 128), F32),
        dma((2, 2, m)),
        dma((2, m)),
        dma((2, m)),
        dma((2, 2, 2)),
        dma((2, 2, 2)),
        dma((10,)),
        dma((10,)),
        dma((2, 2, m, 4)),
        dma((2, 2, m, 4)),
        pltpu.VMEM((9 * local, chans), F32),
    ] + RingSum.scratch(n, rest // (RINGS * n), True)
    outs += [((8, 128), F32), ((8, 128), F32), ((rest, 128), BF16)]
    out_any = [len(outs) - 1]
    packable = local % 128 == 0
    block = 9 * chans * local // 128
    if packable:
        grain = RINGS * n * 16
        taps = -(-4 * block // grain) * grain
        scratch += [pltpu.VMEM((taps, 128), BF16)]
        scratch += RingSum.scratch(n, taps // (RINGS * n), False)
        out_any.append(len(outs))
        outs.append(((taps, 128), BF16))
    else:
        outs += [
            ((2, 9, chans, local), BF16),
            ((2, chans // 128, 9 * local, 128), BF16),
        ]
    kernel = partial(conv_kernel, n, m, split, packable)
    results = vmem_call(kernel, outs, scratch, 4, "res_blocks", in_any, out_any)(*args)
    if packable:
        parts = [results[-1][at * block : (at + 1) * block] for at in range(4)]
        ones, twos = parts[::2], parts[1::2]
    else:
        ones, twos = lax.psum((results[-2], results[-1]), "seq")
    ones = [part.reshape(3, 3, chans, local).astype(F32) for part in ones]
    twos = [part.reshape(chans // 128, 3, 3, local, 128) for part in twos]
    twos = [jnp.concatenate(list(part), axis=-1).astype(F32) for part in twos]
    return results[:7], ones, twos


def text_grads(prompt, text):
    length, width = prompt.shape
    local = (text.shape[1] - 128) // 2
    block = 512

    def kernel(prompt_ref, text_ref, key_ref, value_ref):
        turned = turn(prompt_ref[...])
        key_ref[...] = dot(turned, text_ref[:, :local])
        value_ref[...] = dot(turned, text_ref[:, local : 2 * local])

    out = jax.ShapeDtypeStruct((width, local), F32)
    return pl.pallas_call(
        kernel,
        grid=(width // block,),
        in_specs=[
            pl.BlockSpec((length, block), lambda i: (0, i)),
            pl.BlockSpec(text.shape, lambda i: (0, 0)),
        ],
        out_specs=[pl.BlockSpec((block, local), lambda i: (i, 0))] * 2,
        out_shape=[out, out],
        compiler_params=pltpu.CompilerParams(vmem_limit_bytes=VMEM_LIMIT),
        name="text_grads",
    )(prompt, text)


def time_features(steps, width):
    half = width // 2
    freqs = jnp.exp(-math.log(10000.0) * jnp.arange(half, dtype=jnp.float32) / half)
    angles = steps.astype(jnp.float32)[:, None] * freqs[None, :]
    return jax.nn.silu(jnp.concatenate([jnp.cos(angles), jnp.sin(angles)], axis=1))


def on_device(
    tokens,
    prompt_embed,
    out_grad,
    norm_self,
    w_query,
    w_key,
    w_value,
    w_out,
    norm_cross,
    c_query,
    c_key,
    c_value,
    c_out,
    norm_feed,
    w_up,
    b_up,
    w_down,
    b_down,
    timesteps,
    crop_feats,
    crop_grad_in,
    crop_gain_one,
    crop_conv_one,
    crop_time,
    crop_gain_two,
    crop_conv_two,
    mid_feats,
    mid_grad_in,
    mid_gain_one,
    mid_conv_one,
    mid_time,
    mid_gain_two,
    mid_conv_two,
):
    n, m = lax.axis_size("seq"), lax.axis_size("mp")
    x = tokens[0]
    h1, qh, kv, log, ah, mix = attn_forward(
        x, norm_self[None], w_query, w_key, w_value, n
    )
    peers = []
    for values in (crop_feats, crop_grad_in, mid_feats, mid_grad_in):
        peers.append(
            [
                lax.ppermute(values[0], "mp", [((i + d) % m, i) for i in range(m)])
                for d in range(1, m)
            ]
        )
    mix, peers = lax.optimization_barrier((mix, peers))
    prompt = prompt_embed[0]
    keys_two = dot(prompt, c_key).astype(BF16)
    values_two = dot(prompt, c_value).astype(BF16)
    (
        base,
        units_sum,
        after,
        ga,
        text,
        packed,
    ) = middle(
        mix,
        x,
        out_grad[0],
        w_out,
        norm_cross[None],
        c_query,
        keys_two,
        values_two,
        c_out,
        norm_feed[None],
        w_up,
        b_up[None],
        w_down,
        b_down[None],
        n,
        m,
    )
    local_width = w_query.shape[1]
    features = time_features(timesteps, crop_time.shape[0])
    split = packed_split(local_width, w_up.shape[1], n)[0]
    grad_tokens, output, grad_norm_self, text_sum, packed, first_part = attn_backward(
        ga,
        qh,
        kv,
        log,
        ah,
        h1,
        x,
        norm_self[None],
        w_query,
        w_key,
        w_value,
        after,
        base,
        units_sum,
        text,
        packed,
        w_up.shape[1],
        n,
        m,
    )
    if text.shape[0] % (8 * n):
        text_sum = lax.psum(text, "seq").astype(BF16)
    grad_ckey, grad_cvalue = text_grads(prompt, text_sum)
    features = time_features(timesteps, crop_time.shape[0])
    (
        (crop_out, grad_crop, mid_out, grad_mid, conv_vec, norm_self_sum, second_part),
        (crop_cone, mid_cone),
        (crop_ctwo, mid_ctwo),
    ) = (
        res_blocks(
        (
            (
                crop_feats,
                crop_grad_in,
                crop_gain_one,
                crop_conv_one,
                crop_time,
                crop_gain_two,
                crop_conv_two,
            ),
            (
                mid_feats,
                mid_grad_in,
                mid_gain_one,
                mid_conv_one,
                mid_time,
                mid_gain_two,
                mid_conv_two,
            ),
        ),
        features,
        packed,
        grad_norm_self,
        split,
        peers,
        n,
        m,
    ))
    (
        grad_cquery,
        grad_cout,
        grad_out,
        grad_up,
        grad_down,
        grad_query,
        grad_key,
        grad_value,
    ) = unpack(first_part, second_part, local_width, w_up.shape[1])
    joined = text_sum[:, 2 * local_width :].astype(F32).reshape(-1)
    sizes = (D, D, w_up.shape[1], D)
    ends = [sum(sizes[: i + 1]) for i in range(len(sizes))]
    norm_cross_sum, norm_feed_sum, up_bias_sum, down_bias_sum = [
        joined[end - size : end] for size, end in zip(sizes, ends)
    ]
    norm_self_sum = norm_self_sum.reshape(-1)
    crop_gone, crop_gtwo, crop_hid, mid_gone, mid_gtwo, mid_hid = conv_vec[
        :6, : crop_gain_one.shape[0]
    ]

    def time_grad(sums):
        return features.T * sums[None, :]

    return (
        output[None],
        grad_tokens[None],
        norm_self_sum,
        grad_query,
        grad_key,
        grad_value,
        grad_out,
        norm_cross_sum,
        grad_cquery,
        grad_ckey,
        grad_cvalue,
        grad_cout,
        norm_feed_sum,
        grad_up,
        up_bias_sum,
        grad_down,
        down_bias_sum,
        crop_out[None],
        grad_crop[None],
        crop_gone,
        crop_cone,
        time_grad(crop_hid),
        crop_gtwo,
        crop_ctwo,
        mid_out[None],
        grad_mid[None],
        mid_gone,
        mid_cone,
        time_grad(mid_hid),
        mid_gtwo,
        mid_ctwo,
    )


def solution(mesh):
    in_specs = (
        P(None, "seq", None),
        P(),
        P(None, "seq", None),
        P(),
        P(None, "mp"),
        P(None, "mp"),
        P(None, "mp"),
        P("mp", None),
        P(),
        P(None, "mp"),
        P(None, "mp"),
        P(None, "mp"),
        P("mp", None),
        P(),
        P(None, "mp"),
        P("mp"),
        P("mp", None),
        P(),
        P(),
        P(None, "seq", "mp", None),
        P(None, "seq", "mp", None),
        P("mp"),
        P(None, None, None, "mp"),
        P(None, "mp"),
        P("mp"),
        P(None, None, "mp", None),
        P(None, "seq", "mp", None),
        P(None, "seq", "mp", None),
        P("mp"),
        P(None, None, None, "mp"),
        P(None, "mp"),
        P("mp"),
        P(None, None, "mp", None),
    )
    out_specs = (
        P(None, "seq", None),
        P(None, "seq", None),
        P(),
        P(None, "mp"),
        P(None, "mp"),
        P(None, "mp"),
        P("mp", None),
        P(),
        P(None, "mp"),
        P(None, "mp"),
        P(None, "mp"),
        P("mp", None),
        P(),
        P(None, "mp"),
        P("mp"),
        P("mp", None),
        P(),
        P(None, "seq", "mp", None),
        P(None, "seq", "mp", None),
        P("mp"),
        P(None, None, None, "mp"),
        P(None, "mp"),
        P("mp"),
        P(None, None, "mp", None),
        P(None, "seq", "mp", None),
        P(None, "seq", "mp", None),
        P("mp"),
        P(None, None, None, "mp"),
        P(None, "mp"),
        P("mp"),
        P(None, None, "mp", None),
    )
    return jax.shard_map(
        on_device, mesh=mesh, in_specs=in_specs, out_specs=out_specs, check_vma=False
    )
```

```python
from functools import partial
import math

import jax
import jax.numpy as jnp
from jax import lax
from jax.experimental import pallas as pl
from jax.experimental.pallas import tpu as pltpu
from jax.sharding import PartitionSpec as P

D = 1024
HEADS = 16
GROUPS = 32
E = D // HEADS
SCALE = E ** (-0.5)
COEF = SCALE * math.log2(math.e)
KEY_CHUNK = 512
VMEM_LIMIT = 60 * 1024 * 1024
RINGS = 4

HIGHEST = lax.Precision.HIGHEST
MESH = pl.DeviceIdType.MESH
F32 = jnp.float32
BF16 = jnp.bfloat16


def dot(left, right):
    return jnp.dot(left, right, preferred_element_type=F32)


def dot_nt(left, right):
    return lax.dot_general(left, right, (((1,), (1,)), ((), ())), preferred_element_type=F32)


def dot_tn(left, right):
    return lax.dot_general(left, right, (((0,), (0,)), ((), ())), preferred_element_type=F32)


def wrap(value, size):
    value = jnp.where(value < 0, value + size, value)
    return jnp.where(value >= size, value - size, value)


def turn(block):
    return block.astype(F32).T.astype(BF16)


def greet(peers):
    barrier = pltpu.get_barrier_semaphore()
    for peer in peers:
        pl.semaphore_signal(barrier, inc=1, device_id=peer, device_id_type=MESH)
    pl.semaphore_wait(barrier, len(peers))


def remote(src, dst, send_sem, recv_sem, peer):
    return pltpu.make_async_remote_copy(
        src_ref=src,
        dst_ref=dst,
        send_sem=send_sem,
        recv_sem=recv_sem,
        device_id=peer,
        device_id_type=MESH,
    )


def vmem_call(kernel, outs, scratch, collective_id, name, in_any=(), out_any=(), aliases=None):
    def call(*args):
        return pl.pallas_call(
            kernel,
            out_shape=[jax.ShapeDtypeStruct(shape, kind) for shape, kind in outs],
            in_specs=[
                pl.BlockSpec(memory_space=pl.ANY if i in in_any else pltpu.VMEM)
                for i in range(len(args))
            ],
            out_specs=[
                pl.BlockSpec(memory_space=pl.ANY if i in out_any else pltpu.VMEM)
                for i in range(len(outs))
            ],
            scratch_shapes=scratch,
            input_output_aliases=aliases or {},
            compiler_params=pltpu.CompilerParams(
                collective_id=collective_id,
                has_side_effects=True,
                vmem_limit_bytes=VMEM_LIMIT,
            ),
            name=name,
        )(*args)

    return call


def norm_parts(values):
    center = values - jnp.mean(values, axis=-1, keepdims=True)
    inverse = lax.rsqrt(jnp.mean(center * center, axis=-1, keepdims=True) + 1e-05)
    return center * inverse, inverse


def norm_back(grad, normed, inverse, gain):
    gain_grad = jnp.sum(grad * normed, axis=0, keepdims=True)
    scaled = grad * gain
    first = jnp.mean(scaled, axis=-1, keepdims=True)
    second = jnp.mean(scaled * normed, axis=-1, keepdims=True)
    return inverse * (scaled - first - normed * second), gain_grad


class Exchange:
    def __init__(self, land, send_sem, recv_sem, m):
        self.land, self.send_sem, self.recv_sem, self.m = land, send_sem, recv_sem, m
        self.me = lax.axis_index("mp")

    def peer(self, d):
        return lax.rem(self.me + d, self.m)

    def send(self, key, rows, block):
        self.land[key, self.me, rows, :] = block.astype(BF16)
        for d in range(1, self.m):
            to = self.peer(d)
            part = self.land.at[key, self.me, rows, :]
            remote(
                part, part, self.send_sem.at[key, d], self.recv_sem.at[key, self.me], {"mp": to}
            ).start()

    def wait(self, key, rows):
        for d in range(1, self.m):
            src = self.peer(d)
            part = self.land.at[key, src, rows, :]
            copy = remote(
                part, part, self.send_sem.at[key, d], self.recv_sem.at[key, src], {"mp": src}
            )
            copy.wait_send()
            copy.wait_recv()
        total = self.land[key, 0, rows, :].astype(F32)
        for j in range(1, self.m):
            total = total + self.land[key, j, rows, :].astype(F32)
        return total


def head_peers(h, g):
    me = lax.axis_index("seq")
    slot, part = lax.div(me, g), lax.rem(me, g)
    swaps = [({"seq": lax.rem(slot + d, h) * g + part}) for d in range(1, h)]
    mates = [({"seq": slot * g + lax.rem(part + d, g)}) for d in range(1, g)]
    return slot, part, swaps, mates


def lanes(index, size):
    return pl.ds(pl.multiple_of(index * size, size), size)


class Swap:
    def __init__(self, h, g, send_sem, recv_sem):
        self.h, self.g = h, g
        self.slot, self.part, _, _ = head_peers(h, g)
        self.send_sem, self.recv_sem = send_sem, recv_sem

    def other(self, d):
        return lax.rem(self.slot + d, self.h)

    def device(self, slot):
        return {"seq": slot * self.g + self.part}


def spread_heads(swap, key, source, land, width, offset):
    for d in range(1, swap.h):
        to = swap.other(d)
        remote(
            source.at[pl.ds(pl.multiple_of(to * E, E), E), :],
            land.at[:, lanes(offset + swap.slot, width)],
            swap.send_sem.at[key, d],
            swap.recv_sem.at[key, swap.slot],
            swap.device(to),
        ).start()
    land[:, lanes(offset + swap.slot, width)] = source[
        pl.ds(pl.multiple_of(swap.slot * E, E), E), :
    ]


def spread_wait(swap, key, source, land, width, offset):
    for d in range(1, swap.h):
        src = swap.other(d)
        copy = remote(
            source.at[pl.ds(pl.multiple_of(src * E, E), E), :],
            land.at[:, lanes(offset + src, width)],
            swap.send_sem.at[key, d],
            swap.recv_sem.at[key, src],
            swap.device(src),
        )
        copy.wait_send()
        copy.wait_recv()


def return_copy(swap, key, piece, land, to):
    return remote(
        piece,
        land.at[pl.ds(pl.multiple_of(swap.slot * E, E), E), :],
        swap.send_sem.at[key, to],
        swap.recv_sem.at[key, swap.slot],
        swap.device(to),
    )


def return_wait(swap, key, pieces, land):
    for d in range(1, swap.h):
        src = swap.other(d)
        copy = remote(
            pieces.at[src],
            land.at[pl.ds(pl.multiple_of(src * E, E), E), :],
            swap.send_sem.at[key, src],
            swap.recv_sem.at[key, src],
            swap.device(src),
        )
        copy.wait_send()
        copy.wait_recv()


def mate_copy(part_to, key, d, src, dst, send_sem, recv_sem, slot, part, g):
    return remote(
        src, dst, send_sem.at[key, d], recv_sem.at[key, part], {"seq": slot * g + part_to}
    )


def attn_forward_kernel(
    h,
    g,
    x_ref,
    gain_ref,
    wq_ref,
    wk_ref,
    wv_ref,
    h1_ref,
    qh_ref,
    kv_ref,
    log_ref,
    ah_ref,
    mix_ref,
    local,
    q_land,
    kv_land,
    keys,
    mix_land,
    pieces,
    send_sem,
    recv_sem,
    mate_send,
    mate_recv,
):
    tokens = x_ref.shape[0]
    width = h * tokens
    slot, part, swaps, mates = head_peers(h, g)
    greet(swaps + mates)
    swap = Swap(h, g, send_sem, recv_sem)

    normed, _ = norm_parts(x_ref[...].astype(F32))
    first = (normed * gain_ref[...]).astype(BF16)
    h1_ref[...] = first
    for key, weight in enumerate((wk_ref, wv_ref, wq_ref)):
        local[key] = dot(first, weight[...]).T.astype(BF16)
        if key < 2:
            spread_heads(swap, key, local.at[key], kv_land.at[key], tokens, part * h)
        else:
            spread_heads(swap, key, local.at[key], q_land, tokens, 0)

    for key in range(2):
        spread_wait(swap, key, local.at[key], kv_land.at[key], tokens, part * h)
        mine = kv_land.at[key, :, lanes(part, width)]
        for d in range(1, g):
            mate_copy(
                lax.rem(part + d, g), key, d, mine, mine, mate_send, mate_recv, slot, part, g
            ).start()
    spread_wait(swap, 2, local.at[2], q_land, tokens, 0)
    for key in range(2):
        for d in range(1, g):
            src = lax.rem(part + d, g)
            theirs = kv_land.at[key, :, lanes(src, width)]
            copy = remote(
                theirs,
                theirs,
                mate_send.at[key, d],
                mate_recv.at[key, src],
                {"seq": slot * g + src},
            )
            copy.wait_send()
            copy.wait_recv()

    chunks = g * width // KEY_CHUNK

    @pl.loop(0, chunks)
    def _(c):
        keys[lanes(c, KEY_CHUNK), :] = turn(kv_land[0, :, lanes(c, KEY_CHUNK)])

    @pl.loop(0, h)
    def _(b):
        at = lax.rem(slot + 1 + b, h)
        query = q_land[:, lanes(at, tokens)]

        def step(c, carry):
            peak, total, acc = carry
            scores = dot(keys[lanes(c, KEY_CHUNK), :], query)
            higher = jnp.maximum(peak, jnp.max(scores, axis=0, keepdims=True))
            probs = jnp.exp2((scores - higher) * COEF)
            shrink = jnp.exp2((peak - higher) * COEF)
            total = total * shrink + jnp.sum(probs, axis=0, keepdims=True)
            acc = acc * shrink + dot(kv_land[1, :, lanes(c, KEY_CHUNK)], probs.astype(BF16))
            return higher, total, acc

        start = (
            jnp.full((1, tokens), -jnp.inf, F32),
            jnp.zeros((1, tokens), F32),
            jnp.zeros((E, tokens), F32),
        )
        peak, total, acc = lax.fori_loop(0, chunks, step, start)
        mixed = acc / total
        log_ref[at] = peak * COEF + jnp.log2(total)
        ah_ref[:, lanes(at, tokens)] = mixed
        pieces[at] = mixed.astype(BF16)

        @pl.when(b < h - 1)
        def _():
            return_copy(swap, 3, pieces.at[at], mix_land, at).start()

    mix_land[pl.ds(pl.multiple_of(slot * E, E), E), :] = pieces[slot]
    qh_ref[...] = q_land[...]
    kv_ref[...] = kv_land[...]
    return_wait(swap, 3, pieces, mix_land)
    mix_ref[...] = mix_land[...]


def attn_forward(tokens, gain, wq, wk, wv, n):
    rows, local = tokens.shape[0], wq.shape[1]
    h = local // E
    g = n // h
    width = h * rows
    return vmem_call(
        partial(attn_forward_kernel, h, g),
        [
            ((rows, D), BF16),
            ((E, width), BF16),
            ((2, E, g * width), BF16),
            ((h, 1, rows), F32),
            ((E, width), F32),
            ((local, rows), BF16),
        ],
        [
            pltpu.VMEM((3, local, rows), BF16),
            pltpu.VMEM((E, width), BF16),
            pltpu.VMEM((2, E, g * width), BF16),
            pltpu.VMEM((g * width, E), BF16),
            pltpu.VMEM((local, rows), BF16),
            pltpu.VMEM((h, E, rows), BF16),
            pltpu.SemaphoreType.DMA((4, h)),
            pltpu.SemaphoreType.DMA((4, h)),
            pltpu.SemaphoreType.DMA((2, g)),
            pltpu.SemaphoreType.DMA((2, g)),
        ],
        1,
        "attn_forward",
    )(tokens, gain, wq, wk, wv)


class SeqSum:
    def __init__(self, source, land, total, send_sem, recv_sem, n):
        self.source, self.land, self.total = source, land, total
        self.send_sem, self.recv_sem, self.n = send_sem, recv_sem, n
        self.rows = source.shape[0] // n
        self.fits = source.shape[0] % (8 * n) == 0
        self.me = lax.axis_index("seq")

    def block(self, at):
        return pl.ds(pl.multiple_of(at * self.rows, 8), self.rows)

    def back_copy(self, there, owner):
        part = self.total.at[self.block(owner)]
        return remote(part, part, self.send_sem.at[1], self.recv_sem.at[1], {"seq": there})

    def scatter(self):
        @pl.loop(1, self.n)
        def _(d):
            there = wrap(self.me + d, self.n)
            remote(
                self.source.at[self.block(there)],
                self.land.at[self.me],
                self.send_sem.at[0],
                self.recv_sem.at[0],
                {"seq": there},
            ).start()

        self.land[self.me] = self.source[self.block(self.me), :]

    def gather(self):
        rest = pl.ds(0, self.n - 1)
        copy = remote(
            self.land.at[rest],
            self.land.at[rest],
            self.send_sem.at[0],
            self.recv_sem.at[0],
            {"seq": self.me},
        )
        copy.wait_send()
        copy.wait_recv()
        total = self.land[0]
        for j in range(1, self.n):
            total = total + self.land[j]
        self.total[self.block(self.me), :] = total

        @pl.loop(1, self.n)
        def _(d):
            self.back_copy(wrap(self.me + d, self.n), self.me).start()

    def finish(self):
        part = self.total.at[pl.ds(0, (self.n - 1) * self.rows)]
        copy = remote(part, part, self.send_sem.at[1], self.recv_sem.at[1], {"seq": self.me})
        copy.wait_send()
        copy.wait_recv()


def attn_backward_kernel(
    h,
    g,
    m,
    units,
    ga_ref,
    qh_ref,
    kv_ref,
    log_ref,
    ah_ref,
    h1_ref,
    x_ref,
    gain_ref,
    wq_ref,
    wk_ref,
    wv_ref,
    after_ref,
    base_ref,
    partial_ref,
    text_ref,
    _,
    out_ref,
    final_ref,
    dgain_ref,
    text_out_ref,
    packed_ref,
    done_ref,
    ga_land,
    rows_kv,
    sums,
    pieces,
    halves,
    half_land,
    kv_pieces,
    land,
    cross,
    send_sem,
    recv_sem,
    mate_send,
    mate_recv,
    cross_send,
    cross_recv,
    text_land,
    text_total,
    text_send,
    text_recv,
    dqkv,
    dqkv_sem,
    *ring_scratch,
):
    tokens = x_ref.shape[0]
    width = h * tokens
    n = h * g
    local = ga_ref.shape[0]
    slot, part, swaps, mates = head_peers(h, g)
    me, here = lax.axis_index("seq"), lax.axis_index("mp")
    greet(
        [{"seq": lax.rem(me + d, n)} for d in range(1, n)]
        + [{"mp": lax.rem(here + d, m)} for d in range(1, m)]
    )
    swap = Swap(h, g, send_sem, recv_sem)
    mp_sum = Exchange(cross, cross_send, cross_recv, m)

    spread_heads(swap, 0, ga_ref, ga_land, tokens, 0)
    everything = pl.ds(0, tokens)
    mp_sum.send(1, everything, partial_ref[...])
    piece = done_ref.shape[0] // (RINGS * n)
    ring = RingSum(n, piece, True, packed_ref, done_ref, ring_scratch)
    ring.start()
    text_sum = SeqSum(text_ref, text_land, text_total, text_send, text_recv, n)
    if text_sum.fits:
        text_sum.scatter()
    chunks = g * width // KEY_CHUNK

    @pl.loop(0, chunks)
    def _(c):
        for key in range(2):
            rows_kv[key, lanes(c, KEY_CHUNK), :] = turn(kv_ref[key, :, lanes(c, KEY_CHUNK)])
            sums[key, lanes(c, KEY_CHUNK), :] = jnp.zeros((KEY_CHUNK, E), F32)

    spread_wait(swap, 0, ga_ref, ga_land, tokens, 0)
    ring.first()
    in_loop = chunks % 2 == 0 and 2 * h <= ring.ticks_all
    ring.next = 2 * h if in_loop else 0

    def one_block(b):
        at = lax.rem(slot + 1 + b, h)
        query = qh_ref[:, lanes(at, tokens)]
        grad = ga_land[:, lanes(at, tokens)]
        query_rows, grad_rows = turn(query), turn(grad)
        level = log_ref[at]
        inner = jnp.sum(grad.astype(F32) * ah_ref[:, lanes(at, tokens)], axis=0, keepdims=True)

        def step(c, acc):
            here_rows = lanes(c, KEY_CHUNK)
            scores = dot(rows_kv[0, here_rows, :], query)
            probs = jnp.exp2(scores * COEF - level)
            grad_probs = dot(rows_kv[1, here_rows, :], grad)
            grad_scores = (probs * (grad_probs - inner)).astype(BF16)
            sums[0, here_rows, :] += dot(grad_scores, query_rows)
            sums[1, here_rows, :] += dot(probs.astype(BF16), grad_rows)
            return acc + dot(kv_ref[0, :, here_rows], grad_scores)

        acc = jnp.zeros((E, tokens), F32)
        for k in range(2):
            acc = lax.fori_loop(k * chunks // 2, (k + 1) * chunks // 2, step, acc)
            if in_loop:
                ring.tick(2 * b + k)
        pieces[at] = (acc * SCALE).astype(BF16)

        @pl.when(b < h - 1)
        def _():
            return_copy(swap, 1, pieces.at[at], land.at[0], at).start()

    pl.loop(0, h)(one_block)

    for key, factor in ((0, SCALE), (1, 1.0)):
        for d in range(1, g):
            to = lax.rem(part + d, g)

            @pl.loop(0, h)
            def _(i):
                block = sums[key, lanes(to * h + i, tokens), :] * factor
                halves[key, d, :, lanes(i, tokens)] = block.T.astype(BF16)

            remote(
                halves.at[key, d],
                half_land.at[key, part],
                mate_send.at[key, d],
                mate_recv.at[key, part],
                {"seq": slot * g + to},
            ).start()
    if text_sum.fits:
        text_sum.gather()
    ring.idle(3)
    for key, factor in ((0, SCALE), (1, 1.0)):
        for d in range(1, g):
            src = lax.rem(part + d, g)
            copy = remote(
                halves.at[key, d],
                half_land.at[key, src],
                mate_send.at[key, d],
                mate_recv.at[key, src],
                {"seq": slot * g + src},
            )
            copy.wait_send()
            copy.wait_recv()

        @pl.loop(0, h)
        def _(b):
            at = lax.rem(slot + 1 + b, h)
            total = (sums[key, lanes(part * h + at, tokens), :] * factor).T
            for d in range(1, g):
                src = lax.rem(part + d, g)
                total = total + half_land[key, src, :, lanes(at, tokens)].astype(F32)
            kv_pieces[key, at] = total.astype(BF16)

            @pl.when(b < h - 1)
            def _():
                return_copy(swap, 2 + key, kv_pieces.at[key, at], land.at[1 + key], at).start()

    mine = pl.ds(pl.multiple_of(slot * E, E), E)
    land[0, mine, :] = pieces[slot]
    land[1, mine, :] = kv_pieces[0, slot]
    land[2, mine, :] = kv_pieces[1, slot]
    ring.idle(3)
    return_wait(swap, 1, pieces, land.at[0])
    return_wait(swap, 2, kv_pieces.at[0], land.at[1])
    return_wait(swap, 3, kv_pieces.at[1], land.at[2])

    grads = [turn(land[key]) for key in range(3)]
    partial_sum = dot_nt(grads[0], wq_ref[...])
    partial_sum = partial_sum + dot_nt(grads[1], wk_ref[...])
    partial_sum = partial_sum + dot_nt(grads[2], wv_ref[...])
    mp_sum.send(0, everything, partial_sum)
    first = turn(h1_ref[...])
    for key in range(3):
        product = dot(first, grads[key]).astype(BF16)
        for k in range(local // 128):
            row = (key * (local // 128) + k) * D
            dqkv[row : row + D, :] = product[:, k * 128 : (k + 1) * 128]
    start = packed_sections(local, 0)[3][0] + 2 * D // 128 * units
    store = pltpu.make_async_copy(
        dqkv, packed_ref.at[pl.ds(start, dqkv.shape[0])], dqkv_sem.at[0]
    )
    store.start()
    if text_sum.fits:
        text_sum.finish()
        text_out_ref[...] = text_total[...].astype(BF16)
    else:
        text_out_ref[...] = text_ref[...].astype(BF16)
    ring.idle(4)
    final_ref[...] = (base_ref[...] + mp_sum.wait(1, everything)).astype(BF16)
    normed, inverse = norm_parts(x_ref[...].astype(F32))
    total = mp_sum.wait(0, everything)
    into, gain_grad = norm_back(total, normed, inverse, gain_ref[...])
    out_ref[...] = after_ref[...] + into
    dgain_ref[...] = gain_grad
    store.wait()
    ring.finish()


def attn_backward(ga, qh, kv, log, ah, h1, tokens, gain, wq, wk, wv, after, base, partial_out, text, packed, units, n, m):
    rows, local = tokens.shape[0], wq.shape[1]
    h = local // E
    g = n // h
    width = h * rows
    split, total = packed_split(local, units, n)
    return vmem_call(
        partial(attn_backward_kernel, h, g, m, units),
        [
            ((rows, D), F32),
            ((rows, D), BF16),
            ((1, D), F32),
            (text.shape, BF16),
            (packed.shape, BF16),
            ((split, 128), BF16),
        ],
        [
            pltpu.VMEM((E, width), BF16),
            pltpu.VMEM((2, g * width, E), BF16),
            pltpu.VMEM((2, g * width, E), F32),
            pltpu.VMEM((h, E, rows), BF16),
            pltpu.VMEM((2, g, E, width), BF16),
            pltpu.VMEM((2, g, E, width), BF16),
            pltpu.VMEM((2, h, E, rows), BF16),
            pltpu.VMEM((3, local, rows), BF16),
            pltpu.VMEM((2, m, rows, D), BF16),
            pltpu.SemaphoreType.DMA((4, h)),
            pltpu.SemaphoreType.DMA((4, h)),
            pltpu.SemaphoreType.DMA((2, g)),
            pltpu.SemaphoreType.DMA((2, g)),
            pltpu.SemaphoreType.DMA((2, m)),
            pltpu.SemaphoreType.DMA((2, m)),
            pltpu.VMEM((n, max(text.shape[0] // n, 8), text.shape[1]), F32),
            pltpu.VMEM(text.shape, F32),
            pltpu.SemaphoreType.DMA((2,)),
            pltpu.SemaphoreType.DMA((2,)),
            pltpu.VMEM((3 * local // 128 * D, 128), BF16),
            pltpu.SemaphoreType.DMA((1,)),
        ]
        + RingSum.scratch(n, split // (RINGS * n), True),
        2,
        "attn_backward",
        in_any=(15,),
        out_any=(4, 5),
        aliases={15: 4},
    )(ga, qh, kv, log, ah, h1, tokens, gain, wq, wk, wv, after, base, partial_out, text, packed)


def middle_kernel(
    m,
    mix_ref,
    x_ref,
    og_ref,
    wo_ref,
    gain2_ref,
    cq_ref,
    k2_ref,
    v2_ref,
    co_ref,
    gain3_ref,
    wu_ref,
    bu_ref,
    wd_ref,
    bd_ref,
    base_ref,
    units_sum_ref,
    after_ref,
    ga_ref,
    text_ref,
    packed_ref,
    dgain2_ref,
    dgain3_ref,
    dup_ref,
    ddown_ref,
    h2_ref,
    gq2_ref,
    a2_ref,
    go2_ref,
    go_ref,
    h3_ref,
    gz_ref,
    u_ref,
    packed,
    packed_sem,
    back_units,
    x1,
    x2,
    q2,
    probs,
    kd,
    kdt,
    vd,
    vdt,
    land,
    send_sem,
    recv_sem,
):
    here = lax.axis_index("mp")
    greet([{"mp": lax.rem(here + d, m)} for d in range(1, m)])
    mp_sum = Exchange(land, send_sem, recv_sem, m)
    total_rows = x_ref.shape[0]
    rows = total_rows // 2
    blocks = [pl.ds(b * rows, rows) for b in range(2)]
    full = pl.ds(0, rows)
    text, local = k2_ref.shape
    units = wu_ref.shape[1]
    pairs = local // 128
    chunk = min(512, units)

    mixed = turn(mix_ref[...])
    for b in range(2):
        mp_sum.send(b, full, dot(mixed[b * rows : (b + 1) * rows], wo_ref[...]))

    low_lane = lax.broadcasted_iota(jnp.int32, (text, 128), 1) < E
    for p in range(pairs):
        cols = slice(p * 128, (p + 1) * 128)
        for source, plain, turned in ((k2_ref, kd, kdt), (v2_ref, vd, vdt)):
            both = source[:, cols].astype(F32)
            stacked = jnp.concatenate(
                [jnp.where(low_lane, both, 0.0), jnp.where(low_lane, 0.0, both)], axis=0
            )
            plain[p] = stacked.astype(BF16)
            turned[p] = stacked.T.astype(BF16)

    ddown_ref[...] = jnp.sum(og_ref[...].astype(F32), axis=0, keepdims=True)
    for b in range(2):

        @pl.loop(0, units // chunk)
        def _(c):
            cols = lanes(c, chunk)
            back_units[blocks[b], cols] = dot_nt(og_ref[blocks[b], :], wd_ref[cols, :])

    for b in range(2):
        at = blocks[b]
        x1[at, :] = x_ref[at, :].astype(F32) + mp_sum.wait(b, full)
        normed, _ = norm_parts(x1[at, :])
        second = (normed * gain2_ref[...]).astype(BF16)
        h2_ref[at, :] = second
        q2[at, :] = dot(second, cq_ref[...]).astype(BF16)
        for p in range(pairs):
            cols = slice(p * 128, (p + 1) * 128)
            scores = dot(q2[at, cols], kdt[p]) * SCALE
            parts = []
            for i in range(2):
                one = scores[:, i * text : (i + 1) * text]
                expo = jnp.exp(one - jnp.max(one, axis=-1, keepdims=True))
                parts.append(expo / jnp.sum(expo, axis=-1, keepdims=True))
            prob = jnp.concatenate(parts, axis=1)
            probs[p, at, :] = prob
            a2_ref[at, cols] = dot(prob.astype(BF16), vd[p]).astype(BF16)
        mp_sum.send(2 + b, full, dot(a2_ref[at, :], co_ref[...]))

    for b in range(2):
        at = blocks[b]
        x2[at, :] = x1[at, :] + mp_sum.wait(2 + b, full)
        normed, _ = norm_parts(x2[at, :])
        h3_ref[at, :] = (normed * gain3_ref[...]).astype(BF16)

        @pl.loop(0, units // chunk)
        def _(c):
            cols = lanes(c, chunk)
            z = dot(h3_ref[at, :], wu_ref[:, cols]) + bu_ref[:, cols]
            cdf = 0.5 + 0.5 * lax.erf(z * math.sqrt(0.5))
            slope = cdf + z * (jnp.exp(z * z * -0.5) * (1.0 / math.sqrt(2.0 * math.pi)))
            u_ref[at, cols] = (z * cdf).astype(BF16)
            gz = (back_units[at, cols] * slope).astype(BF16)
            gz_ref[at, cols] = gz
            bias = jnp.sum(gz.astype(F32), axis=0, keepdims=True)
            if b == 0:
                dup_ref[:, cols] = bias
            else:
                dup_ref[:, cols] += bias

        mp_sum.send(4 + b, full, dot_nt(gz_ref[at, :], wu_ref[...]))

    for b in range(2):
        at = blocks[b]
        units_sum_ref[at, :] = dot(u_ref[at, :], wd_ref[...]).astype(BF16)
        base_ref[at, :] = x2[at, :] + bd_ref[...]

    sections = packed_sections(local, units)[:5]

    def section_copy(which):
        start, count = sections[which][0], sections[which][1] * sections[which][2]
        rows_here = pl.ds(start, count)
        return pltpu.make_async_copy(
            packed.at[rows_here], packed_ref.at[rows_here], packed_sem.at[which]
        )

    def weight_grad(which, left, right_ref):
        start, count, height = sections[which]
        step = 4 if count % 4 == 0 else 1

        @pl.loop(0, count // step)
        def _(c):
            product = dot(left, right_ref[:, lanes(c, step * 128)]).astype(BF16)
            for k in range(step):
                place = pl.multiple_of(start + (c * step + k) * height, 16)
                packed[pl.ds(place, height), :] = product[:, k * 128 : (k + 1) * 128]

        section_copy(which).start()

    weight_grad(3, turn(h3_ref[...]), gz_ref)
    weight_grad(4, turn(u_ref[...]), og_ref)

    for b in range(2):
        at = blocks[b]
        normed, inverse = norm_parts(x2[at, :])
        into, gain_grad = norm_back(mp_sum.wait(4 + b, full), normed, inverse, gain3_ref[...])
        after = og_ref[at, :].astype(F32) + into
        x2[at, :] = after
        go2 = after.astype(BF16)
        go2_ref[at, :] = go2
        ga2 = dot_nt(go2, co_ref[...]).astype(BF16)
        for p in range(pairs):
            cols = slice(p * 128, (p + 1) * 128)
            prob = probs[p, at, :]
            grad_prob = dot(ga2[:, cols], vdt[p])
            parts = []
            for i in range(2):
                half = slice(i * text, (i + 1) * text)
                one, grad_one = prob[:, half], grad_prob[:, half]
                inner = jnp.sum(one * grad_one, axis=-1, keepdims=True)
                parts.append(one * (grad_one - inner))
            grad_scores = jnp.concatenate(parts, axis=1)
            gq2_ref[at, cols] = (dot(grad_scores.astype(BF16), kd[p]) * SCALE).astype(BF16)
            both = dot(grad_scores.T.astype(BF16), q2[at, cols]) * SCALE
            key_part = jnp.where(low_lane, both[:text], both[text:])
            both = dot(prob.T.astype(BF16), ga2[:, cols])
            value_part = jnp.where(low_lane, both[:text], both[text:])
            late = slice(local + p * 128, local + (p + 1) * 128)
            if b == 0:
                text_ref[:, cols] = key_part
                text_ref[:, late] = value_part
            else:
                text_ref[:, cols] += key_part
                text_ref[:, late] += value_part
        mp_sum.send(6 + b, full, dot_nt(gq2_ref[at, :], cq_ref[...]))
        if b == 0:
            dgain3_ref[...] = gain_grad
        else:
            dgain3_ref[...] += gain_grad

    weight_grad(0, turn(h2_ref[...]), gq2_ref)
    weight_grad(1, turn(a2_ref[...]), go2_ref)
    for b in range(2):
        at = blocks[b]
        normed, inverse = norm_parts(x1[at, :])
        into, gain_grad = norm_back(mp_sum.wait(6 + b, full), normed, inverse, gain2_ref[...])
        after = x2[at, :] + into
        after_ref[at, :] = after
        go = after.astype(BF16)
        go_ref[at, :] = go
        ga_ref[:, b * rows : (b + 1) * rows] = dot_nt(go, wo_ref[...]).T.astype(BF16)
        if b == 0:
            dgain2_ref[...] = gain_grad
        else:
            dgain2_ref[...] += gain_grad
    weight_grad(2, mix_ref[...], go_ref)
    extra = slice(2 * local, 2 * local + 128)
    text_ref[:, extra] = jnp.zeros((text, 128), F32)
    row = 0
    for vector in (dgain2_ref, dgain3_ref, dup_ref, ddown_ref):
        for i in range(vector.shape[1] // 128):
            text_ref[row : row + 1, extra] = vector[:, i * 128 : (i + 1) * 128]
            row += 1
    for which in range(len(sections)):
        section_copy(which).wait()


def packed_sections(local, units):
    sections, start = [], 0
    for count, height in (
        (local // 128, D),
        (D // 128, local),
        (D // 128, local),
        (units // 128, D),
        (D // 128, units),
        (local // 128, D),
        (local // 128, D),
        (local // 128, D),
    ):
        sections.append((start, count, height))
        start += count * height
    return sections


def packed_split(local, units, n):
    start, count, height = packed_sections(local, units)[-1]
    grain = RINGS * n * 16
    total = -(-(start + count * height) // grain) * grain
    start, count, height = packed_sections(local, units)[2]
    return max((start + count * height) // grain, 1) * grain, total


def unpack(first, second, local, units):
    split = first.shape[0]
    parts = []
    for start, count, height in packed_sections(local, units):
        if start + count * height <= split:
            part = first[start : start + count * height]
        elif start >= split:
            part = second[start - split : start - split + count * height]
        else:
            part = jnp.concatenate([first[start:], second[: start - split + count * height]])
        part = part.reshape(count, height, 128)
        parts.append(part.transpose(1, 0, 2).reshape(height, count * 128).astype(F32))
    return parts


def middle(mix, tokens, og, wo, gain2, cq, k2, v2, co, gain3, wu, bu, wd, bd, n, m):
    rows, (text, local), units = tokens.shape[0], k2.shape, wu.shape[1]
    pairs = local // 128
    _, total = packed_split(local, units, n)
    mine = packed_sections(local, units)[5][0]
    return vmem_call(
        partial(middle_kernel, m),
        [
            ((rows, D), F32),
            ((rows, D), BF16),
            ((rows, D), F32),
            ((local, rows), BF16),
            ((text, 2 * local + 128), F32),
            ((total, 128), BF16),
        ],
        [
            pltpu.VMEM((1, D), F32),
            pltpu.VMEM((1, D), F32),
            pltpu.VMEM((1, units), F32),
            pltpu.VMEM((1, D), F32),
            pltpu.VMEM((rows, D), BF16),
            pltpu.VMEM((rows, local), BF16),
            pltpu.VMEM((rows, local), BF16),
            pltpu.VMEM((rows, D), BF16),
            pltpu.VMEM((rows, D), BF16),
            pltpu.VMEM((rows, D), BF16),
            pltpu.VMEM((rows, units), BF16),
            pltpu.VMEM((rows, units), BF16),
            pltpu.VMEM((mine, 128), BF16),
            pltpu.SemaphoreType.DMA((5,)),
            pltpu.VMEM((rows, units), F32),
            pltpu.VMEM((rows, D), F32),
            pltpu.VMEM((rows, D), F32),
            pltpu.VMEM((rows, local), BF16),
            pltpu.VMEM((pairs, rows, 2 * text), F32),
            pltpu.VMEM((pairs, 2 * text, 128), BF16),
            pltpu.VMEM((pairs, 128, 2 * text), BF16),
            pltpu.VMEM((pairs, 2 * text, 128), BF16),
            pltpu.VMEM((pairs, 128, 2 * text), BF16),
            pltpu.VMEM((8, m, rows // 2, D), BF16),
            pltpu.SemaphoreType.DMA((8, m)),
            pltpu.SemaphoreType.DMA((8, m)),
        ],
        3,
        "middle",
        out_any=(5,),
    )(mix, tokens, og, wo, gain2, cq, k2, v2, co, gain3, wu, bu, wd, bd)


def ring_chip(place, chips):
    if chips % 2:
        return place
    half = chips // 2
    return jnp.where(place < half, 2 * place, 2 * (chips - 1 - place) + 1)


def ring_place(chip, chips):
    if chips % 2:
        return chip
    z, x = lax.div(chip, 2), lax.rem(chip, 2)
    return jnp.where(x == 0, z, chips - 1 - z)


class RingSum:
    SCRATCH = (
        "pair",
        "land",
        "stage",
        "send_sem",
        "recv_sem",
        "pair_send",
        "pair_recv",
        "out_send",
        "out_recv",
        "stage_sem",
        "keep_sem",
    )

    @staticmethod
    def scratch(n, piece, staged):
        dma, chips = pltpu.SemaphoreType.DMA, n // 2
        return [
            pltpu.VMEM((RINGS, chips, piece, 128), BF16),
            pltpu.VMEM((RINGS, chips - 1, piece, 128), BF16),
            pltpu.VMEM((RINGS, 2, piece, 128) if staged else (1, 1, 16, 128), BF16),
            dma((RINGS, 2 * chips)),
            dma((RINGS, 2 * chips)),
            dma((RINGS, chips)),
            dma((RINGS, chips)),
            dma((RINGS, chips)),
            dma((RINGS, chips)),
            dma((RINGS, 2)),
            dma((RINGS,)),
        ]

    def __init__(self, n, piece, staged, own, done, scratch, base=0):
        self.__dict__.update(zip(self.SCRATCH, scratch))
        self.own, self.done, self.base = own, done, base
        self.piece, self.staged = piece, staged
        self.chips, self.steps = n // 2, n // 2 - 1
        me = lax.axis_index("seq")
        chip, self.core = lax.div(me, 2), lax.rem(me, 2)
        place = ring_place(chip, self.chips)
        self.mate = {"seq": 2 * chip + 1 - self.core}
        after = 2 * ring_chip(wrap(place + 1, self.chips), self.chips) + self.core
        before = 2 * ring_chip(wrap(place - 1, self.chips), self.chips) + self.core
        self.ways = [
            (place, {"seq": after}),
            (wrap(self.chips - place, self.chips), {"seq": before}),
        ]
        self.half = RINGS * self.chips * piece
        self.groups = RINGS // 2
        self.next = 0
        self.ticks_all = self.groups * (2 * self.steps - 1)

    def chunk(self, v, t):
        return wrap(v - t, self.chips)

    def rows(self, core, q, chunk, base=0):
        start = base + core * self.half + (q * self.chips + chunk) * self.piece
        return pl.ds(pl.multiple_of(start, 16), self.piece)

    def ring_copy(self, src, dst, q, t, to):
        return remote(src, dst, self.send_sem.at[q, t], self.recv_sem.at[q, t], to)

    def pair_copy(self, q, v, t):
        chunk = self.chunk(v, t)
        return remote(
            self.own.at[self.rows(1 - self.core, q, chunk, self.base)],
            self.pair.at[q, chunk],
            self.pair_send.at[q, t],
            self.pair_recv.at[q, t],
            self.mate,
        )

    def out_copy(self, src, there, q, k):
        return remote(src, there, self.out_send.at[q, k], self.out_recv.at[q, k], self.mate)

    def fetch(self, q, v, t, slot):
        return pltpu.make_async_copy(
            self.own.at[self.rows(self.core, q, self.chunk(v, t), self.base)],
            self.stage.at[q, slot],
            self.stage_sem.at[q, slot],
        )

    def keep(self, q, v):
        return pltpu.make_async_copy(
            self.land.at[q, self.steps - 1],
            self.done.at[self.rows(self.core, q, wrap(v + 1, self.chips))],
            self.keep_sem.at[q],
        )

    def mine(self, q, v, t, slot):
        chunk = self.chunk(v, t)
        if self.staged:
            self.fetch(q, v, t, slot).wait()
            part = self.stage[q, slot]
        else:
            part = self.own[self.rows(self.core, q, chunk, self.base), :]
        self.pair_copy(q, v, t).wait_recv()
        return part.astype(F32) + self.pair[q, chunk].astype(F32)

    def start(self):
        for t in range(2):
            for q in range(RINGS):
                v, _ = self.ways[q % 2]
                self.pair_copy(q, v, t).start()
                if self.staged:
                    self.fetch(q, v, t, t).start()

    def first(self):
        for q in range(RINGS):
            v, to = self.ways[q % 2]
            here = self.pair.at[q, v]
            self.pair[q, v] = self.mine(q, v, 0, 0).astype(BF16)
            self.ring_copy(here, self.land.at[q, 0], q, 0, to).start()

    def tick(self, u):
        steps = self.steps
        t = lax.div(u, self.groups) + 1
        group = lax.rem(u, self.groups)
        slot = lax.rem(t, 2)

        @pl.when(t <= steps)
        def _():
            for way in range(2):
                v, to = self.ways[way]
                q = 2 * group + way

                @pl.when(t < steps)
                def _():
                    self.pair_copy(q, v, t + 1).start()
                    if self.staged:
                        self.fetch(q, v, t + 1, 1 - slot).start()

                here = self.land.at[q, t - 1]
                mine = self.mine(q, v, t, slot)
                self.ring_copy(here, here, q, t - 1, to).wait_recv()
                self.land[q, t - 1] = (self.land[q, t - 1].astype(F32) + mine).astype(BF16)

                @pl.when(t < steps)
                def _():
                    self.ring_copy(here, self.land.at[q, t], q, t, to).start()

                @pl.when(t == steps)
                def _():
                    there = self.done.at[self.rows(self.core, q, wrap(v + 1, self.chips))]
                    self.ring_copy(here, there, q, t, to).start()
                    self.out_copy(here, there, q, 0).start()
                    self.keep(q, v).start()

        @pl.when(t > steps)
        def _():
            for way in range(2):
                v, to = self.ways[way]
                q = 2 * group + way
                k = t - steps
                part = self.done.at[self.rows(self.core, q, self.chunk(v + 1, k))]
                self.ring_copy(part, part, q, t - 1, to).wait_recv()
                self.ring_copy(part, part, q, t, to).start()
                self.out_copy(part, part, q, k).start()

    def loop(self, count, ticks, body):
        ticks = max(min(ticks, self.ticks_all - self.next, count), 0)
        if ticks == 0:
            pl.loop(0, count)(body)
            return
        first = self.next
        self.next += ticks
        every = count // ticks

        @pl.loop(0, ticks)
        def _(k):
            @pl.loop(0, every)
            def _(i):
                body(k * every + i)

            self.tick(first + k)

        if ticks * every < count:
            pl.loop(ticks * every, count)(body)

    def idle(self, count):
        count = min(count, self.ticks_all - self.next)
        first = self.next
        self.next += count
        if count:
            pl.loop(first, first + count)(self.tick)

    def finish(self):
        self.idle(self.ticks_all)
        last = 2 * self.steps
        for q in range(RINGS):
            v, to = self.ways[q % 2]
            part = self.done.at[self.rows(self.core, q, self.chunk(v + 1, self.steps))]
            self.ring_copy(part, part, q, last - 1, to).wait_recv()
            self.out_copy(part, part, q, self.steps).start()
            self.keep(q, v).wait()

        @pl.loop(0, last)
        def _(t):
            for q in range(RINGS):
                v, to = self.ways[q % 2]
                self.ring_copy(self.land.at[q, 0], self.land.at[q, 0], q, t, to).wait_send()

        @pl.loop(0, self.chips)
        def _(t):
            for q in range(RINGS):
                v, _ = self.ways[q % 2]
                self.pair_copy(q, v, t).wait_send()
                other = self.done.at[self.rows(1 - self.core, q, self.chunk(v + 1, t))]
                copy = self.out_copy(other, other, q, t)
                copy.wait_send()
                copy.wait_recv()


GROUP = 8


def fold(values):
    total = values[:, :128]
    for i in range(1, values.shape[1] // 128):
        total = total + values[:, i * 128 : (i + 1) * 128]
    return total


def wide(columns, width):
    return jnp.concatenate([columns] * (width // 128), axis=1) if width > 128 else columns


def silu_parts(scaled):
    gate = jax.nn.sigmoid(scaled)
    return scaled * gate, gate * (1.0 + scaled * (1.0 - gate))


def pack_sums(columns):
    lane = lax.broadcasted_iota(jnp.int32, (8, 128), 1)
    tile = jnp.zeros((8, 128), F32)
    for q, sums in enumerate(columns):
        groups = sums.shape[0] // GROUP
        line = jnp.sum(sums, axis=1, keepdims=True)
        for t in range(groups):
            tile = jnp.where(lane == q * groups + t, line[t * GROUP : (t + 1) * GROUP], tile)
    return tile


def unpack_sums(tile, count, channels):
    groups = channels // GROUP
    row = jnp.sum(tile, axis=0, keepdims=True)
    turned = jnp.broadcast_to(row, (128, 128)).T
    blocks = []
    for q in range(count):
        part = turned[q * groups : (q + 1) * groups]
        part = jnp.broadcast_to(part[:, None, :], (groups, GROUP, 128))
        blocks.append(part.reshape(channels, 128))
    return blocks


def put_shifted(stack, row, values):
    width = values.shape[1]
    lane = lax.broadcasted_iota(jnp.int32, values.shape, 1)
    stack[row, 0] = jnp.where(lane == 0, 0.0, pltpu.roll(values, 1, 1)).astype(BF16)
    stack[row, 1] = values.astype(BF16)
    stack[row, 2] = jnp.where(lane == width - 1, 0.0, pltpu.roll(values, width - 1, 1)).astype(BF16)


def three_rows(stack, row):
    return stack[pl.ds(row, 3)].reshape(9 * stack.shape[2], stack.shape[3])


class ConvMap:
    INPUTS = ("gain_one", "gain_two", "shift", "weight_one", "weight_two")
    OUTPUTS = ("out", "grad")
    SCRATCH = (
        "feats",
        "cot",
        "act",
        "stack_two",
        "wt1",
        "wt2",
        "wb2",
        "wb1",
        "raw",
        "hid",
        "send_both",
        "got_two",
        "got_one",
        "gains",
        "norm_one",
        "norm_two",
        "acc",
        "vec",
    )

    def __init__(self, index, n, m, sources, refs, sems):
        self.index, self.n, self.m = index, n, m
        self.sources = sources
        self.__dict__.update(refs)
        self.__dict__.update(sems)
        self.rows, self.local, self.width = self.out.shape
        self.chans = self.feats.shape[1]
        self.me, self.here = lax.axis_index("seq"), lax.axis_index("mp")
        self.high = self.rows * n
        self.count = float(self.high * self.width * GROUP)
        self.own = pl.ds(pl.multiple_of(self.here * self.local, self.local), self.local)
        self.step = max(self.rows // 4, 2)

    def ticks(self, crop, mid):
        return (crop, mid)[self.index]

    def peer(self, d):
        return lax.rem(self.here + d, self.m)

    def loads(self, which):
        full = (self.feats, self.cot)[which]
        copies = []
        for d in range(self.m):
            chans = pl.ds(pl.multiple_of(self.peer(d) * self.local, self.local), self.local)
            copies.append(
                pltpu.make_async_copy(
                    self.sources[which][d],
                    full.at[pl.ds(2, self.rows), chans, :],
                    self.load_sem.at[self.index, which, d],
                )
            )
        return copies

    def gain_copies(self):
        return [
            remote(
                self.gain_one,
                self.gains.at[self.own, :],
                self.gain_send.at[self.index, d],
                self.gain_recv.at[self.index, d],
                {"mp": self.peer(d)},
            )
            for d in range(1, self.m)
        ]

    def edges(self, which):
        full, rows = (self.feats, self.cot)[which], self.rows
        up = remote(
            full.at[pl.ds(2, 2)],
            full.at[pl.ds(rows + 2, 2)],
            self.edge_send.at[self.index, which, 0],
            self.edge_recv.at[self.index, which, 0],
            {"seq": jnp.maximum(self.me - 1, 0)},
        )
        down = remote(
            full.at[pl.ds(rows, 2)],
            full.at[pl.ds(0, 2)],
            self.edge_send.at[self.index, which, 1],
            self.edge_recv.at[self.index, which, 1],
            {"seq": jnp.minimum(self.me + 1, self.n - 1)},
        )
        return up, down

    def start_edges(self, which):
        up, down = self.edges(which)
        full, rows = (self.feats, self.cot)[which], self.rows
        blank = jnp.zeros((2,) + full.shape[1:], BF16)

        @pl.when(self.me > 0)
        def _():
            up.start()

        @pl.when(self.me == 0)
        def _():
            full[pl.ds(0, 2)] = blank

        @pl.when(self.me < self.n - 1)
        def _():
            down.start()

        @pl.when(self.me == self.n - 1)
        def _():
            full[pl.ds(rows + 2, 2)] = blank

    def wait_edges(self, which):
        up, down = self.edges(which)

        @pl.when(self.me > 0)
        def _():
            up.wait_send()
            down.wait_recv()

        @pl.when(self.me < self.n - 1)
        def _():
            down.wait_send()
            up.wait_recv()

    def stat_copy(self, key, part, there):
        return remote(
            part, part, self.stat_send.at[key], self.stat_recv.at[key], {"seq": there}
        )

    def send_stats(self, e, tile):
        key = 4 * self.index + e
        self.stat[key, self.me] = tile

        @pl.loop(1, self.n)
        def _(d):
            part = self.stat.at[key, self.me]
            self.stat_copy(key, part, wrap(self.me + d, self.n)).start()

    def sum_stats(self, e):
        key = 4 * self.index + e
        copy = self.stat_copy(key, self.stat.at[key, pl.ds(0, self.n - 1)], self.me)
        copy.wait_send()
        copy.wait_recv()
        total = self.stat[key, 0]
        for j in range(1, self.n):
            total = total + self.stat[key, j]
        return total

    def wait_stats(self, e, channels):
        return unpack_sums(self.sum_stats(e), 2, channels)

    def clear(self, count):
        for q in range(count):
            self.acc[q] = jnp.zeros(self.acc.shape[1:], F32)

    def valid(self, row):
        at = self.me * self.rows + row
        return jnp.logical_and(at >= 0, at < self.high)

    def inside(self, e):
        return jnp.logical_and(e >= 1, e <= self.rows).astype(F32)

    def wide(self, columns):
        return wide(columns, self.width)

    def lay_out_weights(self):
        chans, local = self.chans, self.local
        for i in range(3):
            for j in range(3):
                tap = 3 * i + j
                one, two = self.weight_one[i, j], self.weight_two[i, j]
                rows = slice(j * local, (j + 1) * local)
                self.wt1[rows, i * chans : (i + 1) * chans] = turn(one)
                self.wt2[:, tap * local : (tap + 1) * local] = turn(two)
                rows = slice((2 - j) * local, (3 - j) * local)
                self.wb2[rows, (2 - i) * chans : (3 - i) * chans] = two
                self.wb1[:, (8 - tap) * local : (9 - tap) * local] = one

    def row_pairs(self):
        return 256 // self.width if self.width < 256 and self.rows % 2 == 0 else 1

    def conv_all(self, weights, source, ticks, use):
        together, local, width = self.row_pairs(), self.local, self.width
        taps_in = 3 * self.chans

        def body(step):
            first = step * together
            side = [source[pl.ds(first + k, 3)].reshape(taps_in, width) for k in range(together)]
            block = jnp.concatenate(side, axis=1) if together > 1 else side[0]
            products = dot(weights[...], block)
            lane = lax.broadcasted_iota(jnp.int32, (local, width), 1)
            for k in range(together):
                cols = slice(k * width, (k + 1) * width)
                left, middle, right = [
                    products[j * local : (j + 1) * local, cols] for j in range(3)
                ]
                left = jnp.where(lane == 0, 0.0, pltpu.roll(left, 1, 1))
                right = jnp.where(lane == width - 1, 0.0, pltpu.roll(right, width - 1, 1))
                use(first + k, left + middle + right)

        self.back.loop((self.rows + 2) // together, ticks, body)

    def first_sums(self):
        self.clear(2)

        @pl.loop(0, self.rows)
        def _(y):
            values = self.feats[y + 2].astype(F32)
            self.acc[0] += fold(values)
            self.acc[1] += fold(values * values)

        self.send_stats(0, pack_sums([self.acc[0], self.acc[1]]))

    def back_two(self):
        def use(e, values):
            self.raw[e] = values

        self.conv_all(self.wb2, self.cot, self.ticks(4, 1), use)

    def norm_of(self, total, squares):
        mean = total / self.count
        return mean, lax.rsqrt(squares / self.count - mean * mean + 1e-05)

    def conv_one(self):
        mean, inverse = self.norm_of(*self.wait_stats(0, self.chans))
        self.norm_one[0], self.norm_one[1] = mean, inverse
        gains = self.gains[...]
        scale = inverse * gains
        offset = -mean * scale
        self.norm_one[2], self.norm_one[3] = scale, offset

        def activate(r):
            scaled = self.feats[r].astype(F32) * self.wide(self.norm_one[2])
            scaled = scaled + self.wide(self.norm_one[3])
            act = scaled * jax.nn.sigmoid(scaled)
            self.act[r] = jnp.where(self.valid(r - 2), act, 0.0).astype(BF16)

        self.back.loop(self.rows + 4, self.ticks(1, 1), activate)
        self.clear(2)

        def use(e, values):
            hid = values + self.wide(self.shift[...])
            self.hid[e] = hid
            mine = self.inside(e)
            self.acc[0, : self.local] += fold(hid) * mine
            self.acc[1, : self.local] += fold(hid * hid) * mine

        self.conv_all(self.wt1, self.act, self.ticks(4, 1), use)
        self.send_stats(1, pack_sums([self.acc[0, : self.local], self.acc[1, : self.local]]))

    def second_norm(self, e):
        normed = (self.hid[e] - self.wide(self.norm_two[0])) * self.wide(self.norm_two[1])
        return normed, normed * self.wide(self.gain_two[...])

    def conv_two(self):
        mean, inverse = self.norm_of(*self.wait_stats(1, self.local))
        self.norm_two[0], self.norm_two[1] = mean, inverse
        self.clear(2)

        def sweep(e):
            normed, scaled = self.second_norm(e)
            act, slope = silu_parts(scaled)
            put_shifted(self.stack_two, e, jnp.where(self.valid(e - 1), act, 0.0))
            grad = self.raw[e] * slope
            self.raw[e] = grad * self.wide(self.gain_two[...])
            mine = self.inside(e)
            self.acc[0, : self.local] += fold(grad) * mine
            self.acc[1, : self.local] += fold(grad * normed) * mine

        self.back.loop(self.rows + 2, self.ticks(2, 1), sweep)
        first, second = self.acc[0, : self.local], self.acc[1, : self.local]
        self.put_vec(1, second)
        gain = self.gain_two[...]
        self.send_stats(2, pack_sums([first * gain, second * gain]))
        for c in range(self.rows // self.step):

            self.conv_own(self.wt2, self.send_both, c * self.step, self.step)

            for copy in self.channel_copies(0, c):
                copy.start()

        self.weight_sum(self.cot, self.ticks(2, 0))
        for i in range(self.chans // 128):
            cols = slice(i * 128, (i + 1) * 128)
            self.put_taps(2 * self.index + 1, i, self.sums[:, cols].astype(BF16))

    def many_rows(self):
        return min(1024 // self.width, self.rows)

    def put_taps(self, which, block, values):
        if self.last is None:
            (self.gw1, self.gw2)[which % 2][which // 2, block] = values
        else:
            rows = values.shape[0]
            start = which * 9 * self.chans * self.local // 128 + block * rows
            self.taps[start : start + rows, :] = values

    def last_loop(self, count, ticks, body):
        if self.last is not None:
            self.last.loop(count, ticks, body)
        else:
            pl.loop(0, count)(body)

    def side_rows(self, y, together):
        side = [three_rows(self.stack_two, y + k) for k in range(together)]
        return jnp.concatenate(side, axis=1) if together > 1 else side[0]

    def conv_own(self, weights, target, start, count):
        together = self.row_pairs()

        def body(step):
            first = start + step * together
            product = dot(weights[...], self.side_rows(first, together)).astype(BF16)
            for k in range(together):
                target[first + k] = product[:, k * self.width : (k + 1) * self.width]

        self.back.loop(count // together, self.ticks(start // count % 2, start // count // 3), body)

    def put_vec(self, at, columns):
        lane = lax.broadcasted_iota(jnp.int32, (self.local, 128), 1)
        line = jnp.sum(columns, axis=1, keepdims=True)
        self.vec[...] = jnp.where(lane == at, line, self.vec[...])

    def channel_copies(self, which, c):
        out = self.send_both
        land = (self.got_two, self.got_one)[which]
        rows = pl.ds(c * self.step, self.step)
        copies = []
        for d in range(1, self.m):
            to = self.peer(d)
            chans = pl.ds(pl.multiple_of(to * self.local, self.local), self.local)
            copies.append(
                remote(
                    out.at[rows, chans, :],
                    land.at[d - 1, rows],
                    self.chan_send.at[self.index, which, d, c],
                    self.chan_recv.at[self.index, which, d, c],
                    {"mp": to},
                )
            )
        return copies

    def wait_channels(self, which):
        for c in range(self.rows // self.step):
            for copy in self.channel_copies(which, c):
                copy.wait_send()
                copy.wait_recv()

    def channel_sum(self, which, y):
        total = self.send_both[y, self.own, :].astype(F32)
        land = (self.got_two, self.got_one)[which]
        for d in range(1, self.m):
            total = total + land[d - 1, y].astype(F32)
        return total

    def back_one(self):
        first, second = self.wait_stats(2, self.local)
        self.norm_two[2], self.norm_two[3] = first / self.count, second / self.count
        self.acc[2, : self.local] = jnp.zeros((self.local, 128), F32)

        def sweep(e):
            normed, _ = self.second_norm(e)
            grad = self.raw[e] - self.wide(self.norm_two[2]) - normed * self.wide(self.norm_two[3])
            grad = jnp.where(self.valid(e - 1), grad * self.wide(self.norm_two[1]), 0.0)
            put_shifted(self.stack_two, e, grad)
            self.acc[2, : self.local] += fold(grad) * self.inside(e)

        self.back.loop(self.rows + 2, self.ticks(2, 1), sweep)
        self.put_vec(2, self.acc[2, : self.local])
        self.finish_out()
        for c in range(self.rows // self.step):

            self.conv_own(self.wb1, self.send_both, c * self.step, self.step)

            for copy in self.channel_copies(1, c):
                copy.start()

    def grad_weight_one(self):
        self.weight_sum(self.act, self.ticks(2, 0))
        for tap in range(9):
            rows = slice((8 - tap) * self.local, (9 - tap) * self.local)
            self.put_taps(2 * self.index, tap, self.sums[rows, :].T.astype(BF16))

    def weight_sum(self, source, ticks):
        together = self.many_rows()
        self.sums[...] = jnp.zeros(self.sums.shape, F32)

        def body(step):
            first = step * together
            block = jnp.concatenate([source[first + k + 2] for k in range(together)], axis=1)
            self.sums[...] += dot_nt(self.side_rows(first, together), block)

        self.back.loop(self.rows // together, ticks, body)

    def own_norm(self, y):
        mean, inverse = self.norm_one[0, self.own, :], self.norm_one[1, self.own, :]
        values = self.feats[y + 2, self.own, :].astype(F32)
        normed = (values - self.wide(mean)) * self.wide(inverse)
        return values, normed, inverse

    def last_sums(self):
        self.wait_channels(1)
        self.clear(2)

        def sweep(y):
            _, normed, _ = self.own_norm(y)
            _, slope = silu_parts(normed * self.wide(self.gain_one[...]))
            grad = self.channel_sum(1, y) * slope
            self.grad[y] = grad
            self.acc[0, : self.local] += fold(grad)
            self.acc[1, : self.local] += fold(grad * normed)

        self.last_loop(self.rows, self.ticks(5, 2), sweep)
        first, second = self.acc[0, : self.local], self.acc[1, : self.local]
        self.put_vec(0, second)
        gain = self.gain_one[...]
        self.send_stats(3, pack_sums([first * gain, second * gain]))

    def finish_out(self):
        self.wait_channels(0)

        @pl.loop(0, self.rows)
        def _(y):
            values = self.feats[y + 2, self.own, :].astype(F32)
            self.out[y] = (values + self.channel_sum(0, y)).astype(BF16)

    def finish_grad(self):
        first, second = self.wait_stats(3, self.local)
        self.norm_two[2], self.norm_two[3] = first / self.count, second / self.count

        def sweep(y):
            _, normed, inverse = self.own_norm(y)
            grad = self.grad[y] * self.wide(self.gain_one[...])
            grad = grad - self.wide(self.norm_two[2]) - normed * self.wide(self.norm_two[3])
            cot = self.cot[y + 2, self.own, :].astype(F32)
            self.grad[y] = cot + grad * self.wide(inverse)

        self.last_loop(self.rows, self.ticks(5, 2), sweep)


def conv_kernel(n, m, split, packable, *refs):
    refs = list(refs)

    def take(count):
        taken = refs[:count]
        del refs[:count]
        return taken

    own, gain_ref = take(2)
    sources, inputs = [], []
    for _ in range(2):
        sources.append((take(m), take(m)))
        inputs.append(take(len(ConvMap.INPUTS)))
    outputs = [take(len(ConvMap.OUTPUTS)) for _ in range(2)]
    vec_ref, gain_out, done = take(3)
    shared = {"last": None}
    if packable:
        last_done = take(1)[0]
    else:
        shared.update(zip(("gw1", "gw2"), take(2)))
    scratch = [take(len(ConvMap.SCRATCH)) for _ in range(2)]
    names = (
        "stat",
        "load_sem",
        "gain_send",
        "gain_recv",
        "edge_send",
        "edge_recv",
        "stat_send",
        "stat_recv",
        "chan_send",
        "chan_recv",
        "sums",
    )
    shared.update(zip(names, take(len(names))))
    piece = done.shape[0] // (RINGS * n)
    back = RingSum(n, piece, True, own, done, take(len(RingSum.SCRATCH)), split)
    shared["back"] = back
    last = None
    if packable:
        taps = take(1)[0]
        piece = taps.shape[0] // (RINGS * n)
        last = RingSum(n, piece, False, taps, last_done, take(len(RingSum.SCRATCH)))
        shared.update(taps=taps, last=last)
    maps = []
    for i in range(2):
        named = dict(zip(ConvMap.INPUTS, inputs[i]))
        named.update(zip(ConvMap.OUTPUTS, outputs[i]))
        named.update(zip(ConvMap.SCRATCH, scratch[i]))
        maps.append(ConvMap(i, n, m, sources[i], named, shared))

    for one in maps:
        for which in range(2):
            for copy in one.loads(which):
                copy.start()
    me, here = maps[0].me, maps[0].here
    greet(
        [{"seq": lax.rem(me + d, n)} for d in range(1, n)]
        + [{"mp": lax.rem(here + d, m)} for d in range(1, m)]
    )
    for one in maps:
        one.gains[one.own, :] = one.gain_one[...]
        one.vec[...] = jnp.zeros(one.vec.shape, F32)
        for copy in one.gain_copies():
            copy.start()
    for which in (1, 0):
        for one in maps:
            for copy in one.loads(which):
                copy.wait()
            one.start_edges(which)
    back.start()
    maps[1].send_stats(5, gain_ref[...])
    for one in maps:
        one.lay_out_weights()
    for one in maps:
        one.first_sums()
    back.first()
    for one in maps:
        one.wait_edges(1)
        one.back_two()
    for one in maps:
        for copy in one.gain_copies():
            copy.wait_send()
            copy.wait_recv()
        one.wait_edges(0)
        one.conv_one()
    for one in maps:
        one.conv_two()
    for one in maps:
        one.back_one()
    for one in maps:
        one.grad_weight_one()
    if packable:
        rows = 4 * 9 * maps[0].chans * maps[0].local // 128
        if rows < taps.shape[0]:
            taps[rows:, :] = jnp.zeros((taps.shape[0] - rows, 128), BF16)
        last.start()
        last.first()
    back.idle(back.ticks_all)
    for one in maps:
        one.last_sums()
    lines = [one.vec[...].T[:3] for one in maps]
    lines = jnp.concatenate(lines + [jnp.zeros((2, maps[0].local), F32)], axis=0)
    if maps[0].local < 128:
        blank = jnp.zeros((8, 128 - maps[0].local), F32)
        lines = jnp.concatenate([lines, blank], axis=1)
    maps[1].send_stats(4, lines)
    for one in maps:
        one.finish_grad()
    vec_ref[...] = maps[1].sum_stats(4)
    gain_out[...] = maps[1].sum_stats(5)
    back.finish()
    if packable:
        last.finish()


def res_blocks(maps, features, packed, vector, split, peers, n, m):
    args, in_any, outs, scratch = [packed, vector.reshape(8, 128)], [0], [], []
    for feats, cot, gain_one, conv_one, time_weight, gain_two, conv_two in maps:
        _, rows, local, width = feats.shape
        chans = conv_one.shape[2]
        for values in (feats[0], cot[0]):
            in_any += range(len(args), len(args) + m)
            args.append(values)
            args += peers.pop(0)
        shift = jnp.dot(features, time_weight.astype(F32), precision=HIGHEST)[0]
        args += [
            jnp.broadcast_to(column[:, None], (local, 128))
            for column in (gain_one, gain_two, shift)
        ]
        args += [conv_one, conv_two]
        outs += [
            ((rows, local, width), BF16),
            ((rows, local, width), F32),
        ]
        scratch += [
            pltpu.VMEM((rows + 4, chans, width), BF16),
            pltpu.VMEM((rows + 4, chans, width), BF16),
            pltpu.VMEM((rows + 4, chans, width), BF16),
            pltpu.VMEM((rows + 2, 3, local, width), BF16),
            pltpu.VMEM((3 * local, 3 * chans), BF16),
            pltpu.VMEM((chans, 9 * local), BF16),
            pltpu.VMEM((3 * local, 3 * chans), BF16),
            pltpu.VMEM((chans, 9 * local), BF16),
            pltpu.VMEM((rows + 2, local, width), F32),
            pltpu.VMEM((rows + 2, local, width), F32),
            pltpu.VMEM((rows, chans, width), BF16),
            pltpu.VMEM((m - 1, rows, local, width), BF16),
            pltpu.VMEM((m - 1, rows, local, width), BF16),
            pltpu.VMEM((chans, 128), F32),
            pltpu.VMEM((4, chans, 128), F32),
            pltpu.VMEM((4, local, 128), F32),
            pltpu.VMEM((3, chans, 128), F32),
            pltpu.VMEM((local, 128), F32),
        ]
    dma = pltpu.SemaphoreType.DMA
    rest = packed.shape[0] - split
    scratch += [
        pltpu.VMEM((10, n, 8, 128), F32),
        dma((2, 2, m)),
        dma((2, m)),
        dma((2, m)),
        dma((2, 2, 2)),
        dma((2, 2, 2)),
        dma((10,)),
        dma((10,)),
        dma((2, 2, m, 4)),
        dma((2, 2, m, 4)),
        pltpu.VMEM((9 * local, chans), F32),
    ] + RingSum.scratch(n, rest // (RINGS * n), True)
    outs += [((8, 128), F32), ((8, 128), F32), ((rest, 128), BF16)]
    out_any = [len(outs) - 1]
    packable = local % 128 == 0
    block = 9 * chans * local // 128
    if packable:
        grain = RINGS * n * 16
        taps = -(-4 * block // grain) * grain
        scratch += [pltpu.VMEM((taps, 128), BF16)]
        scratch += RingSum.scratch(n, taps // (RINGS * n), False)
        out_any.append(len(outs))
        outs.append(((taps, 128), BF16))
    else:
        outs += [
            ((2, 9, chans, local), BF16),
            ((2, chans // 128, 9 * local, 128), BF16),
        ]
    kernel = partial(conv_kernel, n, m, split, packable)
    results = vmem_call(kernel, outs, scratch, 4, "res_blocks", in_any, out_any)(*args)
    if packable:
        parts = [results[-1][at * block : (at + 1) * block] for at in range(4)]
        ones, twos = parts[::2], parts[1::2]
    else:
        ones, twos = lax.psum((results[-2], results[-1]), "seq")
    ones = [part.reshape(3, 3, chans, local).astype(F32) for part in ones]
    twos = [part.reshape(chans // 128, 3, 3, local, 128) for part in twos]
    twos = [jnp.concatenate(list(part), axis=-1).astype(F32) for part in twos]
    return results[:7], ones, twos


def text_grads(prompt, text):
    length, width = prompt.shape
    local = (text.shape[1] - 128) // 2
    block = 1024

    def kernel(prompt_ref, text_ref, key_ref, value_ref):
        turned = turn(prompt_ref[...])
        key_ref[...] = dot(turned, text_ref[:, :local])
        value_ref[...] = dot(turned, text_ref[:, local : 2 * local])

    out = jax.ShapeDtypeStruct((width, local), F32)
    return pl.pallas_call(
        kernel,
        grid=(width // block,),
        in_specs=[
            pl.BlockSpec((length, block), lambda i: (0, i)),
            pl.BlockSpec(text.shape, lambda i: (0, 0)),
        ],
        out_specs=[pl.BlockSpec((block, local), lambda i: (i, 0))] * 2,
        out_shape=[out, out],
        compiler_params=pltpu.CompilerParams(vmem_limit_bytes=VMEM_LIMIT),
        name="text_grads",
    )(prompt, text)


def time_features(steps, width):
    half = width // 2
    freqs = jnp.exp(-math.log(10000.0) * jnp.arange(half, dtype=jnp.float32) / half)
    angles = steps.astype(jnp.float32)[:, None] * freqs[None, :]
    return jax.nn.silu(jnp.concatenate([jnp.cos(angles), jnp.sin(angles)], axis=1))


def on_device(
    tokens,
    prompt_embed,
    out_grad,
    norm_self,
    w_query,
    w_key,
    w_value,
    w_out,
    norm_cross,
    c_query,
    c_key,
    c_value,
    c_out,
    norm_feed,
    w_up,
    b_up,
    w_down,
    b_down,
    timesteps,
    crop_feats,
    crop_grad_in,
    crop_gain_one,
    crop_conv_one,
    crop_time,
    crop_gain_two,
    crop_conv_two,
    mid_feats,
    mid_grad_in,
    mid_gain_one,
    mid_conv_one,
    mid_time,
    mid_gain_two,
    mid_conv_two,
):
    n, m = lax.axis_size("seq"), lax.axis_size("mp")
    x = tokens[0]
    h1, qh, kv, log, ah, mix = attn_forward(
        x, norm_self[None], w_query, w_key, w_value, n
    )
    peers = []
    for values in (crop_feats, crop_grad_in, mid_feats, mid_grad_in):
        peers.append(
            [
                lax.ppermute(values[0], "mp", [((i + d) % m, i) for i in range(m)])
                for d in range(1, m)
            ]
        )
    mix, peers = lax.optimization_barrier((mix, peers))
    prompt = prompt_embed[0]
    keys_two = dot(prompt, c_key).astype(BF16)
    values_two = dot(prompt, c_value).astype(BF16)
    (
        base,
        units_sum,
        after,
        ga,
        text,
        packed,
    ) = middle(
        mix,
        x,
        out_grad[0],
        w_out,
        norm_cross[None],
        c_query,
        keys_two,
        values_two,
        c_out,
        norm_feed[None],
        w_up,
        b_up[None],
        w_down,
        b_down[None],
        n,
        m,
    )
    local_width = w_query.shape[1]
    features = time_features(timesteps, crop_time.shape[0])
    split = packed_split(local_width, w_up.shape[1], n)[0]
    grad_tokens, output, grad_norm_self, text_sum, packed, first_part = attn_backward(
        ga,
        qh,
        kv,
        log,
        ah,
        h1,
        x,
        norm_self[None],
        w_query,
        w_key,
        w_value,
        after,
        base,
        units_sum,
        text,
        packed,
        w_up.shape[1],
        n,
        m,
    )
    if text.shape[0] % (8 * n):
        text_sum = lax.psum(text, "seq").astype(BF16)
    grad_ckey, grad_cvalue = text_grads(prompt, text_sum)
    features = time_features(timesteps, crop_time.shape[0])
    (
        (crop_out, grad_crop, mid_out, grad_mid, conv_vec, norm_self_sum, second_part),
        (crop_cone, mid_cone),
        (crop_ctwo, mid_ctwo),
    ) = (
        res_blocks(
        (
            (
                crop_feats,
                crop_grad_in,
                crop_gain_one,
                crop_conv_one,
                crop_time,
                crop_gain_two,
                crop_conv_two,
            ),
            (
                mid_feats,
                mid_grad_in,
                mid_gain_one,
                mid_conv_one,
                mid_time,
                mid_gain_two,
                mid_conv_two,
            ),
        ),
        features,
        packed,
        grad_norm_self,
        split,
        peers,
        n,
        m,
    ))
    (
        grad_cquery,
        grad_cout,
        grad_out,
        grad_up,
        grad_down,
        grad_query,
        grad_key,
        grad_value,
    ) = unpack(first_part, second_part, local_width, w_up.shape[1])
    joined = text_sum[:, 2 * local_width :].astype(F32).reshape(-1)
    sizes = (D, D, w_up.shape[1], D)
    ends = [sum(sizes[: i + 1]) for i in range(len(sizes))]
    norm_cross_sum, norm_feed_sum, up_bias_sum, down_bias_sum = [
        joined[end - size : end] for size, end in zip(sizes, ends)
    ]
    norm_self_sum = norm_self_sum.reshape(-1)
    crop_gone, crop_gtwo, crop_hid, mid_gone, mid_gtwo, mid_hid = conv_vec[
        :6, : crop_gain_one.shape[0]
    ]

    def time_grad(sums):
        return features.T * sums[None, :]

    return (
        output[None],
        grad_tokens[None],
        norm_self_sum,
        grad_query,
        grad_key,
        grad_value,
        grad_out,
        norm_cross_sum,
        grad_cquery,
        grad_ckey,
        grad_cvalue,
        grad_cout,
        norm_feed_sum,
        grad_up,
        up_bias_sum,
        grad_down,
        down_bias_sum,
        crop_out[None],
        grad_crop[None],
        crop_gone,
        crop_cone,
        time_grad(crop_hid),
        crop_gtwo,
        crop_ctwo,
        mid_out[None],
        grad_mid[None],
        mid_gone,
        mid_cone,
        time_grad(mid_hid),
        mid_gtwo,
        mid_ctwo,
    )


def solution(mesh):
    in_specs = (
        P(None, "seq", None),
        P(),
        P(None, "seq", None),
        P(),
        P(None, "mp"),
        P(None, "mp"),
        P(None, "mp"),
        P("mp", None),
        P(),
        P(None, "mp"),
        P(None, "mp"),
        P(None, "mp"),
        P("mp", None),
        P(),
        P(None, "mp"),
        P("mp"),
        P("mp", None),
        P(),
        P(),
        P(None, "seq", "mp", None),
        P(None, "seq", "mp", None),
        P("mp"),
        P(None, None, None, "mp"),
        P(None, "mp"),
        P("mp"),
        P(None, None, "mp", None),
        P(None, "seq", "mp", None),
        P(None, "seq", "mp", None),
        P("mp"),
        P(None, None, None, "mp"),
        P(None, "mp"),
        P("mp"),
        P(None, None, "mp", None),
    )
    out_specs = (
        P(None, "seq", None),
        P(None, "seq", None),
        P(),
        P(None, "mp"),
        P(None, "mp"),
        P(None, "mp"),
        P("mp", None),
        P(),
        P(None, "mp"),
        P(None, "mp"),
        P(None, "mp"),
        P("mp", None),
        P(),
        P(None, "mp"),
        P("mp"),
        P("mp", None),
        P(),
        P(None, "seq", "mp", None),
        P(None, "seq", "mp", None),
        P("mp"),
        P(None, None, None, "mp"),
        P(None, "mp"),
        P("mp"),
        P(None, None, "mp", None),
        P(None, "seq", "mp", None),
        P(None, "seq", "mp", None),
        P("mp"),
        P(None, None, None, "mp"),
        P(None, "mp"),
        P("mp"),
        P(None, None, "mp", None),
    )
    return jax.shard_map(
        on_device, mesh=mesh, in_specs=in_specs, out_specs=out_specs, check_vma=False
    )
```
